128 devices in a mesh: rows: 8 (over x, z_hi), cols: 16 (over y, z_lo, core).
Axes of the slice: x: 4, y: 4, z: 4 (z_hi: 2, z_lo: 2; z = z_hi * 2 + z_lo), core: 2. Of those that a mesh axis runs over, the one named last changes fastest.
Arguments:
- grid_token_states: bfloat16 [64, 256, 512], P('rows', 'cols'), may hold values from -6 to 6
- upstream_gradient: bfloat16 [64, 256, 512], P('rows', 'cols'), may hold values from -6 to 6
- noise_level_step: int32 [1], replicated, may hold values from 0 to 999
- picture_category_label: int32 [1], replicated, may hold values from 0 to 999
- category_gain_offset: bfloat16 [1000, 512], replicated, may hold values from -2 to 2
- noise_level_gain_matrix: bfloat16 [256, 512], replicated, may hold values from -0.375 to 0.375
- attention_input_matrix: bfloat16 [512, 1536], replicated, may hold values from -0.25 to 0.25
- final_projection_matrix: bfloat16 [512, 512], replicated, may hold values from -0.25 to 0.25
- cosine_logit_gain: float32 [8], replicated, may hold values from 2 to 160, as said below
Outputs:
- output: bfloat16 [64, 256, 512], P('rows', 'cols')
- grad_latent: bfloat16 [64, 256, 512], P('rows', 'cols')
- qkv_grad: float32 [512, 1536], replicated
- out_grad: float32 [512, 512], replicated
The draws below stay inside these ranges and needn't reach their ends.
Inputs may be any that keep to these rules, and one draw needn't show every extreme that they name: `cosine_logit_gain`: per-head score scale.
All inputs are finite; a program needn't handle non-finite values.
Results may differ from the reference program's by a relative error of at most 0.024.
The reference program's roundings to bfloat16 on the way count: a program that leaves them out, or rounds other values in their place, can miss the bound.
Values may be sent and summed in bfloat16 or wider, within the bound.
No kernel may reach another device: no remote copies, remote signals or barrier semaphores. Data moves between devices by JAX's collectives and lax.ppermute only.
A program may use at most 192 MiB of HBM per device.

```python
import math
import jax
import jax.numpy as jnp
from jax import lax

D = 512
HEADS = 8
HEAD = 64
CLASSES = 1000
FREQS = 256
H_IMG = 64
W_IMG = 256
TOKENS = 16384


def draw_cosine_logit_gain(key, part):
    key = jax.random.fold_in(key, 7)
    lower = jnp.exp(jax.random.uniform(key, (HEADS,), jnp.float32, jnp.log(2.0), jnp.log(40.0)))
    return lower


def steps_of(key, shape, shards, least, top_value):
    def one(position, blocks):
        heights = jax.random.uniform(jax.random.fold_in(jax.random.fold_in(key, 6), position), (blocks,), jnp.float32, least / len(shards), top_value / len(shards))
        return jnp.repeat(jnp.exp(heights), shape[position] // blocks).reshape((-1,) + (1,) * (len(shape) - position - 1))

    factor_of = one(*shards[0])
    for cut in shards[1:]:
        factor_of = factor_of * one(*cut)
    return factor_of


def scatter_about(key, shape, spread, limit, shards=(), kind=jnp.bfloat16):
    loudness = steps_of(key, shape, shards, -0.22, 0.18) if shards else 1.0
    values = jax.random.normal(key, shape, jnp.float32) * spread * loudness
    return jnp.minimum(jnp.maximum(values, -limit), limit).astype(kind)


def setup_inputs(seed: int = 0) -> dict:
    arg_keys = jax.random.split(jax.random.key(seed), 10)
    return {
        "grid_token_states": scatter_about(arg_keys[0], (H_IMG, W_IMG, D), 1.0, 6.0, ((0, 8), (1, 16))),
        "upstream_gradient": scatter_about(arg_keys[1], (H_IMG, W_IMG, D), 1.0, 6.0, ((0, 8), (1, 16))),
        "noise_level_step": jax.random.randint(arg_keys[2], (1,), 0, 1000).astype(jnp.int32),
        "picture_category_label": jax.random.randint(arg_keys[3], (1,), 0, CLASSES).astype(jnp.int32),
        "category_gain_offset": scatter_about(arg_keys[4], (CLASSES, D), 0.3, 2.0),
        "noise_level_gain_matrix": scatter_about(arg_keys[5], (FREQS, D), FREQS ** -0.5, 0.375),
        "attention_input_matrix": scatter_about(arg_keys[6], (D, 3 * D), D ** -0.5, 0.25),
        "final_projection_matrix": scatter_about(arg_keys[7], (D, D), D ** -0.5, 0.25),
        "cosine_logit_gain": draw_cosine_logit_gain(jax.random.fold_in(arg_keys[9], 71), 0),
    }


def cond_scale(noise_level_step, class_row, noise_level_gain_matrix):
    half_freqs = FREQS // 2
    steps_idx = jnp.arange(half_freqs, dtype=jnp.float32)
    freq_rates = 2.0 * math.pi * jnp.exp(steps_idx * (math.log(64.0) / half_freqs))
    angles = noise_level_step[0].astype(jnp.float32) * 0.001 * freq_rates
    features = jnp.concatenate([jnp.cos(angles), jnp.sin(angles)]).astype(jnp.bfloat16)
    shifted = jnp.dot(features[None, :], noise_level_gain_matrix, preferred_element_type=jnp.float32)[0]
    return 1.0 + class_row + shifted

def normalize(content_vector_lines, scale_vec):
    return content_vector_lines * lax.rsqrt(lax.optimization_barrier(jnp.mean(content_vector_lines * content_vector_lines, -1, keepdims=True)) + 1e-06) * scale_vec

def key_values(raw_kv):
    half_width = raw_kv.shape[-1] // 2
    lead_shape = raw_kv.shape[:-1]
    key_part = raw_kv[..., :half_width].reshape(lead_shape + (HEADS, HEAD))
    key_part = key_part * lax.rsqrt(lax.optimization_barrier(jnp.sum(key_part * key_part, -1, keepdims=True)) + 1e-06)
    return jnp.concatenate([key_part.reshape(lead_shape + (half_width,)), raw_kv[..., half_width:]], -1)

def split_per_attention_group(final_mapped_result, cosine_logit_gain):
    model_width = final_mapped_result.shape[-1] // 3
    lead_shape = final_mapped_result.shape[:-1]
    probe_vector_portion = final_mapped_result[..., :model_width].reshape(lead_shape + (HEADS, HEAD))
    probe_vector_portion = probe_vector_portion * lax.rsqrt(lax.optimization_barrier(jnp.sum(probe_vector_portion * probe_vector_portion, -1, keepdims=True)) + 1e-06)
    probe_vector_portion = probe_vector_portion * cosine_logit_gain[:, None]
    return (probe_vector_portion.reshape(lead_shape + (model_width,)), key_values(final_mapped_result[..., model_width:]))

def attend(query_in, keys_in, inside):
    nrows, ncols = (query_in.shape[0], query_in.shape[1])
    model_width = query_in.shape[2]
    query_heads = query_in.reshape(nrows, ncols, HEADS, HEAD)
    logits_all = []
    value_all = []
    for row_off in range(7):
        for col_off in range(7):
            window_kv = keys_in[row_off:row_off + nrows, col_off:col_off + ncols].astype(jnp.bfloat16)
            key_part = window_kv[..., :model_width].reshape(nrows, ncols, HEADS, HEAD)
            value_all.append(window_kv[..., model_width:].reshape(nrows, ncols, HEADS, HEAD))
            logits = jnp.einsum('rchd,rchd->rch', query_heads, key_part, preferred_element_type=jnp.float32)
            mask_here = inside[row_off:row_off + nrows, col_off:col_off + ncols]
            logits_all.append(jnp.where(mask_here[:, :, None], logits, -1e+30))
    logits_all = jnp.stack(logits_all)
    peak = lax.optimization_barrier(jnp.max(logits_all, 0, keepdims=True))
    exponent = jnp.exp(logits_all - peak)
    probability = (exponent / lax.optimization_barrier(jnp.sum(exponent, 0, keepdims=True))).astype(jnp.bfloat16)
    result = jnp.zeros((nrows, ncols, HEADS, HEAD), jnp.float32)
    for offset_idx in range(49):
        result = result + jnp.einsum('rch,rchd->rchd', probability[offset_idx], value_all[offset_idx], preferred_element_type=jnp.float32)
    return result.reshape(nrows, ncols, model_width)

def reference(grid_token_states, upstream_gradient, noise_level_step, picture_category_label, category_gain_offset, noise_level_gain_matrix, attention_input_matrix, final_projection_matrix, cosine_logit_gain):
    height, columns = (grid_token_states.shape[0], grid_token_states.shape[1])
    class_row = category_gain_offset[picture_category_label[0]].astype(jnp.float32)
    scale_vec = cond_scale(noise_level_step, class_row, noise_level_gain_matrix)
    latent32 = grid_token_states.astype(jnp.float32)
    normed32, norm_back = jax.vjp(lambda content_vector_lines: normalize(content_vector_lines, scale_vec), latent32)
    normed = normed32.astype(jnp.bfloat16)
    flat_normed = normed.reshape(-1, D)
    final_mapped_result = jnp.dot(flat_normed, attention_input_matrix, preferred_element_type=jnp.float32).astype(jnp.bfloat16).reshape(height, columns, 3 * D)
    (lone_probe_vector, lone_memory_pair), join_attention_groups = jax.vjp(lambda content_vector_lines: split_per_attention_group(content_vector_lines, cosine_logit_gain), final_mapped_result.astype(jnp.float32))
    queries = lone_probe_vector.astype(jnp.bfloat16)
    keyval = lone_memory_pair.astype(jnp.bfloat16)
    padded = jnp.pad(keyval, ((3, 3), (3, 3), (0, 0)))
    inside = jnp.pad(jnp.ones((height, columns), jnp.float32), 3) > 0.5
    grad_attn = jnp.dot(upstream_gradient.reshape(-1, D), final_projection_matrix.T, preferred_element_type=jnp.float32).reshape(height, columns, D)
    block_rows = math.gcd(height, 8)

    def one_block(rim_carry, block_idx):
        first_row = block_idx * block_rows
        query_blk = lax.dynamic_slice_in_dim(queries, first_row, block_rows, 0)
        keys_blk = lax.dynamic_slice_in_dim(padded, first_row, block_rows + 6, 0).astype(jnp.float32)
        mask_blk = lax.dynamic_slice_in_dim(inside, first_row, block_rows + 6, 0)
        grad_blk = lax.dynamic_slice_in_dim(grad_attn, first_row, block_rows, 0)
        attended_blk, attn_back = jax.vjp(lambda query_in, keys_in: attend(query_in, keys_in, mask_blk), query_blk, keys_blk)
        grad_query_blk, grad_keys_blk = attn_back(grad_blk)
        grad_keys_blk = grad_keys_blk.at[:6].add(rim_carry)
        return (grad_keys_blk[block_rows:], (attended_blk, grad_query_blk, grad_keys_blk[:block_rows]))
    start_carry = jnp.zeros((6, columns + 6, 2 * D), jnp.float32)
    last_rim, (attended, grad_query, grad_keys) = lax.scan(one_block, start_carry, jnp.arange(height // block_rows, dtype=jnp.int32))
    attended = attended.reshape(height, columns, D).astype(jnp.bfloat16)
    grad_query = grad_query.reshape(height, columns, D)
    grad_keys = jnp.concatenate([grad_keys.reshape(height, columns + 6, 2 * D), last_rim], 0)
    grad_keys = grad_keys[3:height + 3, 3:columns + 3]
    grad_proj = join_attention_groups((grad_query.astype(jnp.float32), grad_keys))[0].astype(jnp.bfloat16)
    flat_attended = attended.reshape(-1, D)
    output = (latent32 + jnp.dot(flat_attended, final_projection_matrix, preferred_element_type=jnp.float32).reshape(height, columns, D)).astype(jnp.bfloat16)
    flat_grad = grad_proj.reshape(-1, 3 * D)
    grad_normed = jnp.dot(flat_grad, attention_input_matrix.T, preferred_element_type=jnp.float32).reshape(height, columns, D)
    grad_latent = (upstream_gradient.astype(jnp.float32) + norm_back(grad_normed)[0]).astype(jnp.bfloat16)
    factor = 1.0 / math.sqrt(TOKENS)
    qkv_grad = jnp.dot(flat_normed.T, flat_grad, preferred_element_type=jnp.float32) * factor
    out_grad = jnp.dot(flat_attended.T, upstream_gradient.reshape(-1, D), preferred_element_type=jnp.float32) * factor
    return (output, grad_latent, qkv_grad, out_grad)
```

```python
import functools
import math

import jax
import jax.numpy as jnp
from jax import lax
from jax.experimental import pallas as pl
from jax.experimental.pallas import tpu as pltpu
from jax.sharding import PartitionSpec as P

HEADS = 8
HEAD = 64
BF16 = jnp.bfloat16
F32 = jnp.float32
VMEM_LIMIT = 56 * 1024 * 1024
AXES = ("rows", "cols")
SLOTS = 32
EXT_ROWS = 20
QUERY_ROWS = 14


def mm(a, b):
    return jnp.dot(a, b, preferred_element_type=F32)


def mm_nt(a, b):
    return lax.dot_general(a, b, (((1,), (1,)), ((), ())), preferred_element_type=F32)


def mm_tn(a, b):
    return lax.dot_general(a, b, (((0,), (0,)), ((), ())), preferred_element_type=F32)


def head_sums(product, ones):
    high = product.astype(BF16)
    low = (product - high.astype(F32)).astype(BF16)
    parts = []
    for g in range(2):
        lanes = slice(256 * g, 256 * g + 256)
        parts.append(mm(high[:, lanes], ones) + mm(low[:, lanes], ones))
    return jnp.concatenate(parts, axis=1)


def by_head(block):
    head_of = lax.broadcasted_iota(jnp.int32, block.shape, 1) // HEAD
    zero = jnp.zeros_like(block)
    return jnp.concatenate([jnp.where(head_of == h, block, zero) for h in range(4)], axis=0)


def own_heads(result):
    head_of = lax.broadcasted_iota(jnp.int32, (HEAD, 256), 1) // HEAD
    total = jnp.where(head_of == 0, result[:HEAD], 0.0)
    for h in range(1, 4):
        total = jnp.where(head_of == h, result[HEAD * h : HEAD * (h + 1)], total)
    return total


def main_kernel(
    place_ref, x_ref, du_ref, up_ref, down_ref, left_ref, right_ref, win_ref, wo_ref,
    scale_ref, gain_ref,
    out_ref, dx_ref, send_ref, keep_ref,
    normed_s, du_s, k_s, v_s, q_s, do_s, kraw_s, qraw_s, att_s, dq_s, dk_s, dv_s, kb_s, wb_s, gp_s,
):
    scale = scale_ref[...]
    gain = gain_ref[...]

    def side(ref, row):
        block = ref[16 * (row // 2) : 16 * (row // 2) + 16, :].astype(F32)
        return block[8 * (row % 2) : 8 * (row % 2) + 8]

    def row_of(own, row):
        return jnp.concatenate([own.astype(F32), side(right_ref, row), side(left_ref, row)], axis=0)

    for e in range(EXT_ROWS):
        if e < 6:
            own, row = up_ref[16 * e : 16 * e + 16, :], e
        elif e < 14:
            own, row = x_ref[16 * (e - 6) : 16 * (e - 6) + 16, :], 9 + e - 6
        else:
            own, row = down_ref[16 * (e - 14) : 16 * (e - 14) + 16, :], 25 + e - 14
        x = row_of(own, row)
        r = lax.rsqrt(jnp.mean(x * x, axis=-1, keepdims=True) + 1e-06)
        normed_s[SLOTS * e : SLOTS * (e + 1), :] = (x * r * scale).astype(BF16)
    for f in range(QUERY_ROWS):
        if f < 3:
            own, row = up_ref[16 * (6 + f) : 16 * (7 + f), :], 6 + f
        elif f < 11:
            own, row = du_ref[16 * (f - 3) : 16 * (f - 2), :], 17 + f - 3
        else:
            own, row = down_ref[16 * (6 + f - 11) : 16 * (7 + f - 11), :], 31 + f - 11
        du_s[SLOTS * f : SLOTS * (f + 1), :] = row_of(own, row).astype(BF16)

    same = lax.broadcasted_iota(jnp.int32, (256, 256), 0) // HEAD
    ones = jnp.where(same == lax.broadcasted_iota(jnp.int32, (256, 256), 1) // HEAD, 1.0, 0.0)
    ones = ones.astype(BF16)

    index = lax.broadcasted_iota(jnp.int32, (EXT_ROWS * SLOTS, 128), 0)
    slot = index % SLOTS
    row = index // SLOTS - 6 + place_ref[0]
    col = jnp.where(slot < 24, slot, slot - 32) + place_ref[1]
    inside = (row >= 0) & (row < place_ref[2]) & (col >= 0) & (col < place_ref[3])
    kb_s[...] = jnp.where(inside, 0.0, -1e30)
    index = lax.broadcasted_iota(jnp.int32, (256, 128), 0)
    lane = lax.broadcasted_iota(jnp.int32, (256, 128), 1) % 64
    key_col = jnp.where(index % SLOTS < 24, index % SLOTS, index % SLOTS - 32)
    query_col = jnp.where(lane % SLOTS < 24, lane % SLOTS, lane % SLOTS - 32)
    row_gap = index // SLOTS - lane // SLOTS
    col_gap = key_col - query_col
    near = (row_gap >= 0) & (row_gap <= 6) & (col_gap >= -3) & (col_gap <= 3)
    wb_s[...] = jnp.where(near, 0.0, -1e30)

    for t in range(5):
        rows = slice(128 * t, 128 * t + 128)
        normed = normed_s[rows, :]
        raw = mm(normed, win_ref[:, 512:1024]).astype(BF16)
        kraw_s[rows, :] = raw
        raw = raw.astype(F32)
        k_s[rows, :] = (raw * lax.rsqrt(head_sums(raw * raw, ones) + 1e-06)).astype(BF16)
        v_s[rows, :] = mm(normed, win_ref[:, 1024:1536]).astype(BF16)
    for start, size in ((0, 128), (128, 128), (256, 128), (384, 64)):
        rows = slice(start, start + size)
        raw = mm(normed_s[96 + start : 96 + start + size, :], win_ref[:, 0:512]).astype(BF16)
        qraw_s[rows, :] = raw
        raw = raw.astype(F32)
        q_s[rows, :] = (raw * lax.rsqrt(head_sums(raw * raw, ones) + 1e-06) * gain).astype(BF16)
        do_s[rows, :] = mm_nt(du_s[rows, :], wo_ref[...]).astype(BF16)

    dk_s[...] = jnp.zeros_like(dk_s)
    dv_s[...] = jnp.zeros_like(dv_s)
    for i in range(7):
        keys = slice(64 * i, 64 * i + 256)
        queries = slice(64 * i, 64 * i + 64)
        bias = wb_s[...] + kb_s[keys, :]
        bias = jnp.concatenate([bias, bias], axis=1)
        for g in range(2):
            lanes = slice(256 * g, 256 * g + 256)
            k_t = k_s[keys, lanes]
            v_t = v_s[keys, lanes]
            q_h = by_head(q_s[queries, lanes])
            do_h = by_head(do_s[queries, lanes])
            scores = mm_nt(k_t, q_h) + bias
            weight = jnp.exp(scores - jnp.max(scores, axis=0, keepdims=True))
            weight = weight * (1.0 / jnp.sum(weight, axis=0, keepdims=True))
            prob = weight.astype(BF16)
            dprob = mm_nt(v_t, do_h).astype(BF16).astype(F32)
            mean = jnp.sum(weight * dprob, axis=0, keepdims=True)
            dscore = (weight * (dprob - mean)).astype(BF16)
            low, high = max(2 * i, 6), min(2 * i + 8, 14)
            here = slice((low - 2 * i) * SLOTS, (high - 2 * i) * SLOTS)
            there = slice((low - 6) * SLOTS, (high - 6) * SLOTS)
            dv_s[there, lanes] += mm(prob[here], do_h)
            dk_s[there, lanes] += mm(dscore[here], q_h)
            if 1 <= i <= 5:
                att_s[queries, lanes] = own_heads(mm_tn(prob, v_t)).astype(BF16)
                dq_s[queries, lanes] = own_heads(mm_tn(dscore, k_t)).astype(BF16)

    def own_tokens(ref, first):
        return jnp.concatenate(
            [ref[SLOTS * (first + r) : SLOTS * (first + r) + 16, :] for r in range(8)], axis=0
        )

    att = own_tokens(att_s, 3)
    normed = own_tokens(normed_s, 6)
    x = x_ref[...].astype(F32)
    out_ref[...] = (x + mm(att, wo_ref[...])).astype(BF16)

    def norm_back(raw, grad):
        inv = lax.rsqrt(head_sums(raw * raw, ones) + 1e-06)
        return inv * (grad - raw * (inv * inv) * head_sums(raw * grad, ones))

    dq = norm_back(own_tokens(qraw_s, 3).astype(F32), own_tokens(dq_s, 3).astype(F32) * gain)
    dk = norm_back(own_tokens(kraw_s, 6).astype(F32), own_tokens(dk_s, 0))
    gp_s[:, 0:512] = dq.astype(BF16)
    gp_s[:, 512:1024] = dk.astype(BF16)
    gp_s[:, 1024:1536] = own_tokens(dv_s, 0).astype(BF16)
    dnormed = mm_nt(gp_s[...], win_ref[...]) * scale
    r = lax.rsqrt(jnp.mean(x * x, axis=-1, keepdims=True) + 1e-06)
    along = jnp.mean(dnormed * x, axis=-1, keepdims=True)
    dx = r * dnormed - x * (r * r * r * along)
    dx_ref[...] = (du_ref[...].astype(F32) + dx).astype(BF16)

    for ref in (send_ref, keep_ref):
        ref[:, 0:512] = normed
        ref[:, 1280:1792] = att
    for core in range(2):

        @pl.when(place_ref[4] == core)
        def _():
            for ref, half in ((keep_ref, core), (send_ref, 1 - core)):
                ref[:, 512:1280] = gp_s[:, 768 * half : 768 * half + 768]
                ref[:, 1792:2048] = du_ref[:, 256 * half : 256 * half + 256]


def grads_kernel(factor, keep_ref, got_ref, out_ref):
    def both(first, last):
        return jnp.concatenate([keep_ref[:, first:last], got_ref[:, first:last]], axis=0)

    out_ref[:, 0:768] = (mm_tn(both(0, 512), both(512, 1280)) * factor).astype(BF16)
    out_ref[:, 768:1024] = (mm_tn(both(1280, 1792), both(1792, 2048)) * factor).astype(BF16)


def sum_kernel(rows, parts_ref, out_ref):
    count = parts_ref.shape[0] // rows
    step = max(rows, 16)
    total = parts_ref[0:step, :].astype(F32)
    for i in range(1, count * rows // step):
        total = total + parts_ref[step * i : step * (i + 1), :].astype(F32)
    while total.shape[0] > rows:
        half = total.shape[0] // 2
        total = total[:half] + total[half:]
    block = jnp.concatenate([total] * (step // rows), axis=0).astype(BF16)
    for i in range(count * rows // step):
        out_ref[step * i : step * (i + 1), :] = block


def final_kernel(place_ref, mine_ref, other_ref, qkv_ref, out_ref):
    for core in range(2):

        @pl.when(place_ref[4] == core)
        def _():
            for ref, half in ((mine_ref, core), (other_ref, 1 - core)):
                qkv_ref[:, 768 * half : 768 * half + 768] = ref[:, 0:768].astype(F32)
                out_ref[:, 256 * half : 256 * half + 256] = ref[:, 768:1024].astype(F32)


def call(kernel, outs, scratch=(), flops=0, scalars=0, inputs=0):
    whole = pl.BlockSpec(memory_space=pltpu.VMEM)
    return pl.pallas_call(
        kernel,
        out_shape=outs,
        in_specs=[pl.BlockSpec(memory_space=pltpu.SMEM)] * scalars + [whole] * inputs,
        out_specs=jax.tree.map(lambda _: whole, outs),
        scratch_shapes=list(scratch),
        compiler_params=pltpu.CompilerParams(vmem_limit_bytes=VMEM_LIMIT),
        cost_estimate=pl.CostEstimate(flops=flops, bytes_accessed=4 << 20, transcendentals=0),
    )


def condition(noise_level_step, label, category_gain_offset, noise_level_gain_matrix):
    half_freqs = noise_level_gain_matrix.shape[0] // 2
    steps_idx = jnp.arange(half_freqs, dtype=F32)
    freq_rates = 2.0 * math.pi * jnp.exp(steps_idx * (math.log(64.0) / half_freqs))
    angles = noise_level_step[0].astype(F32) * 0.001 * freq_rates
    features = jnp.concatenate([jnp.cos(angles), jnp.sin(angles)]).astype(BF16)
    shifted = jnp.dot(features[None, :], noise_level_gain_matrix, preferred_element_type=F32)
    class_row = lax.dynamic_slice_in_dim(category_gain_offset, label[0], 1, 0).astype(F32)
    return 1.0 + class_row + shifted


def shifted(value, axis, by):
    count = lax.axis_size(axis)
    pairs = [(i, i + by) for i in range(count) if 0 <= i + by < count]
    return lax.ppermute(value, axis, pairs)


def per_device(
    grid_token_states, upstream_gradient, noise_level_step, picture_category_label,
    category_gain_offset, noise_level_gain_matrix, attention_input_matrix,
    final_projection_matrix, cosine_logit_gain,
):
    x, du = grid_token_states, upstream_gradient
    height, columns, width = x.shape
    n_rows, n_cols = lax.axis_size("rows"), lax.axis_size("cols")
    my_row, my_col = lax.axis_index("rows"), lax.axis_index("cols")

    up = shifted(jnp.concatenate([x[-6:], du[-3:]], axis=0), "rows", 1)
    down = shifted(jnp.concatenate([x[:6], du[:3]], axis=0), "rows", -1)
    scale = condition(
        noise_level_step, picture_category_label, category_gain_offset, noise_level_gain_matrix
    )
    gain = jnp.repeat(cosine_logit_gain, HEAD)[None, :]
    edge = jnp.concatenate([up[:, 8:], x[:, 8:], du[:, 8:], down[:, 8:]], axis=0)
    left = shifted(edge, "cols", 1)
    edge = jnp.concatenate([up[:, :8], x[:, :8], du[:, :8], down[:, :8]], axis=0)
    right = shifted(edge, "cols", -1)

    core = my_col % 2
    place = jnp.stack(
        [my_row * height, my_col * columns, jnp.int32(n_rows * height), jnp.int32(n_cols * columns), core]
    ).astype(jnp.int32)
    tokens = height * columns
    bf = lambda *shape: jax.ShapeDtypeStruct(shape, BF16)
    vm = pltpu.VMEM
    output, grad_latent, send, keep = call(
        main_kernel,
        (bf(tokens, width), bf(tokens, width), bf(tokens, 2048), bf(tokens, 2048)),
        scratch=[
            vm((640, 512), BF16), vm((448, 512), BF16), vm((640, 512), BF16), vm((640, 512), BF16),
            vm((448, 512), BF16), vm((448, 512), BF16), vm((640, 512), BF16), vm((448, 512), BF16),
            vm((448, 512), BF16), vm((448, 512), BF16), vm((256, 512), F32), vm((256, 512), F32),
            vm((640, 128), F32), vm((256, 128), F32), vm((128, 1536), BF16),
        ],
        flops=8 << 30, scalars=1, inputs=10,
    )(
        place, x.reshape(tokens, width), du.reshape(tokens, width), up.reshape(-1, width),
        down.reshape(-1, width), left.reshape(-1, width), right.reshape(-1, width),
        attention_input_matrix, final_projection_matrix, scale, gain,
    )

    swap = [(i, i ^ 1) for i in range(n_cols)]
    got = lax.ppermute(send, "cols", swap)
    factor = 1.0 / math.sqrt(tokens * n_rows * n_cols)
    partial = call(
        functools.partial(grads_kernel, factor), bf(512, 1024), flops=1 << 29, inputs=2
    )(keep, got)

    groups = [
        [r * n_cols + 2 * c + core_ for r in range(n_rows) for c in range(n_cols // 2)]
        for core_ in range(2)
    ]
    members = n_rows * n_cols // 2
    each = 512 // members

    def exchange(value):
        return lax.all_to_all(
            value.reshape(members, each, 1024), AXES, 0, 0, axis_index_groups=groups, tiled=True
        ).reshape(512, 1024)

    summed = call(functools.partial(sum_kernel, each), bf(512, 1024), inputs=1)(exchange(partial))
    mine = exchange(summed)
    other = lax.ppermute(mine, "cols", swap)
    qkv_grad, out_grad = call(
        final_kernel,
        (jax.ShapeDtypeStruct((512, 1536), F32), jax.ShapeDtypeStruct((512, 512), F32)),
        scalars=1, inputs=2,
    )(place, mine, other)
    return output.reshape(x.shape), grad_latent.reshape(x.shape), qkv_grad, out_grad


def solution(mesh):
    placed = (P("rows", "cols", None), P("rows", "cols", None)) + (P(),) * 7
    return jax.shard_map(
        per_device,
        mesh=mesh,
        in_specs=placed,
        out_specs=(P("rows", "cols", None), P("rows", "cols", None), P(), P()),
        check_vma=False,
    )
```

```python
import functools
import math

import jax
import jax.numpy as jnp
from jax import lax
from jax.experimental import pallas as pl
from jax.experimental.pallas import tpu as pltpu
from jax.sharding import PartitionSpec as P

HEADS = 8
HEAD = 64
BF16 = jnp.bfloat16
F32 = jnp.float32
VMEM_LIMIT = 40 * 1024 * 1024
SMALL_LIMIT = 16 * 1024 * 1024
AXES = ("rows", "cols")
NEAR, FAR = 48, 16


def mm(a, b):
    return jnp.dot(a, b, preferred_element_type=F32)


def mm_nt(a, b):
    return lax.dot_general(a, b, (((1,), (1,)), ((), ())), preferred_element_type=F32)


def mm_tn(a, b):
    return lax.dot_general(a, b, (((0,), (0,)), ((), ())), preferred_element_type=F32)


def head_sums(product, ones):
    high = product.astype(BF16)
    low = (product - high.astype(F32)).astype(BF16)
    parts = []
    for g in range(2):
        lanes = slice(256 * g, 256 * g + 256)
        parts.append(mm(high[:, lanes], ones) + mm(low[:, lanes], ones))
    return jnp.concatenate(parts, axis=1)


def by_head(block):
    head_of = lax.broadcasted_iota(jnp.int32, block.shape, 1) // HEAD
    zero = jnp.zeros_like(block)
    return jnp.concatenate([jnp.where(head_of == h, block, zero) for h in range(4)], axis=0)


def own_heads(result):
    head_of = lax.broadcasted_iota(jnp.int32, (32, 256), 1) // HEAD
    total = result[:32]
    for h in range(1, 4):
        total = jnp.where(head_of == h, result[HEAD * h : HEAD * h + 32], total)
    return total


def head_ones():
    row_head = lax.broadcasted_iota(jnp.int32, (256, 256), 0) // HEAD
    lane_head = lax.broadcasted_iota(jnp.int32, (256, 256), 1) // HEAD
    return jnp.where(row_head == lane_head, 1.0, 0.0).astype(BF16)


def lane_gain(gain_ref):
    head_of = lax.broadcasted_iota(jnp.int32, (1, 512), 1) // HEAD
    gain = jnp.zeros((1, 512), F32)
    for h in range(HEADS):
        gain = jnp.where(head_of == h, gain_ref[h], gain)
    return gain


def block(ref, index):
    return ref[16 * index : 16 * index + 16, :].astype(F32)


def tile(ref, index):
    return block(ref, index // 2)[8 * (index % 2) : 8 * (index % 2) + 8]


def normalize(x, scale):
    return x * lax.rsqrt(jnp.mean(x * x, axis=-1, keepdims=True) + 1e-06) * scale


def unit(raw, ones):
    return raw * lax.rsqrt(head_sums(raw * raw, ones) + 1e-06)


def rows_kernel(x_ref, du_ref, c_ref, d_ref, own_ref):
    even = lax.axis_index("rows") % 2 == 0
    own_ref[0:128, :] = x_ref[...]
    own_ref[128:256, :] = du_ref[...]
    for ref, take_last in ((c_ref, even), (d_ref, jnp.logical_not(even))):

        @pl.when(take_last)
        def _():
            ref[0:96, :] = x_ref[32:128, :]
            ref[96:144, :] = du_ref[80:128, :]

        @pl.when(jnp.logical_not(take_last))
        def _():
            ref[0:96, :] = x_ref[0:96, :]
            ref[96:144, :] = du_ref[0:48, :]


def columns_kernel(own_ref, c_ref, d_ref, far_ref, both_ref):
    even = lax.axis_index("rows") % 2 == 0
    first_core = lax.axis_index("cols") % 2 == 0
    sub = lax.broadcasted_iota(jnp.int32, (8, 512), 0)
    both_ref[0:144, :] = c_ref[...]
    both_ref[144:288, :] = d_ref[...]

    def x_edge(x):
        return jnp.where(first_core, x, pltpu.roll(x, 6, 0))[:8]

    def du_edge(du):
        third = jnp.where(first_core, du[2:3], du[15:16])
        return jnp.where(first_core, pltpu.roll(du, 6, 0), pltpu.roll(du, 9, 0))[:8], third

    tiles = []
    thirds = jnp.zeros((8, 512), F32)
    for row in range(8):
        two, third = du_edge(block(own_ref, 8 + row))
        tiles.append(jnp.where(sub < 6, x_edge(block(own_ref, row)), two))
        thirds = jnp.where(sub == row, third, thirds)
    tiles += [thirds, jnp.zeros((8, 512), F32)]
    for ref in (c_ref, d_ref):
        edges = [du_edge(block(ref, 6 + j)) for j in range(3)]
        for j in range(6):
            rest = edges[j][0] if j < 3 else edges[j - 3][1]
            tiles.append(jnp.where(sub < 6, x_edge(block(ref, j)), rest))
    for i in range(11):
        far_ref[16 * i : 16 * i + 16, :] = jnp.concatenate(tiles[2 * i : 2 * i + 2], 0).astype(BF16)


def near_kernel(
    gain_ref, own_ref, mate_ref, c_ref, d_ref, mate_rows_ref, win_ref, wo_ref, scale_ref,
    k_ref, v_ref, q_ref, do_ref, kraw_ref, qraw_ref, normed_ref,
    own_s, mate_s, du_s,
):
    even = lax.axis_index("rows") % 2 == 0
    first_core = lax.axis_index("cols") % 2 == 0
    scale = scale_ref[...]
    gain = lane_gain(gain_ref)
    ones = head_ones()

    def pick(low, high, above):
        return jnp.where(even, high, low) if above else jnp.where(even, low, high)

    def row_parts(row, first):
        if 0 <= row < 8:
            own, mate = block(own_ref, first + row), block(mate_ref, first + row)
        else:
            above = row < 0
            j = (row + (6 if above else -8)) if first == 0 else 6 + (row + (3 if above else -8))
            own = pick(block(c_ref, j), block(d_ref, j), above)
            mate = pick(block(mate_rows_ref, j), block(mate_rows_ref, 9 + j), above)
        return own, jnp.where(first_core, mate[:8], mate[8:])

    for e in range(20):
        own, mate = row_parts(e - 6, 0)
        own_s[16 * e : 16 * e + 16, :] = normalize(own, scale)
        mate_s[8 * e : 8 * e + 8, :] = normalize(mate, scale)
    normed_ref[...] = own_s[96:224, :].astype(BF16)
    for i in range(7):
        first, second = row_parts(2 * i - 3, 8), row_parts(2 * i - 2, 8)
        pair = jnp.concatenate([first[0], second[0], first[1], second[1]], axis=0)
        du_s[NEAR * i : NEAR * (i + 1), :] = pair.astype(BF16)

    def normed_pairs(first_row, count):
        parts = []
        for n in range(count):
            row = first_row + 2 * n
            parts += [own_s[16 * row : 16 * row + 32, :], mate_s[8 * row : 8 * row + 16, :]]
        return jnp.concatenate(parts, axis=0).astype(BF16)

    for t in range(5):
        rows = slice(96 * t, 96 * t + 96)
        normed = normed_pairs(4 * t, 2)
        raw = mm(normed, win_ref[:, 512:1024]).astype(BF16).astype(F32)
        k_ref[rows, :] = unit(raw, ones).astype(BF16)
        v_ref[rows, :] = mm(normed, win_ref[:, 1024:1536]).astype(BF16)
        for n in range(2):
            at = 2 * t + n - 3
            if 0 <= at < 4:
                kraw_ref[32 * at : 32 * at + 32, :] = raw[48 * n : 48 * n + 32].astype(BF16)
    for first, count in ((0, 2), (2, 2), (4, 2), (6, 1)):
        rows = slice(NEAR * first, NEAR * (first + count))
        normed = normed_pairs(3 + 2 * first, count)
        raw = mm(normed, win_ref[:, 0:512]).astype(BF16).astype(F32)
        q_ref[rows, :] = (unit(raw, ones) * gain).astype(BF16)
        do_ref[rows, :] = mm_nt(du_s[rows, :], wo_ref[...]).astype(BF16)
        for n in range(2 * count):
            at = 2 * first + n - 3
            if 0 <= at < 8:
                here = 48 * (n // 2) + 16 * (n % 2)
                qraw_ref[16 * at : 16 * at + 16, :] = raw[here : here + 16].astype(BF16)


def main_kernel(
    gain_ref, own_ref, far_ref, kn_ref, vn_ref, qn_ref, don_ref, kraw_ref, qraw_ref, normed_ref,
    win_ref, wo_ref, scale_ref,
    out_ref, dx_ref, features_ref, send_ref, keep_ref,
    kf_s, vf_s, qf_s, dof_s, att_s, dq_s, dk_s, dv_s, gp_s,
):
    my_row, my_col = lax.axis_index("rows"), lax.axis_index("cols")
    even = my_row % 2 == 0
    first_core = my_col % 2 == 0
    scale = scale_ref[...]
    gain = lane_gain(gain_ref)
    ones = head_ones()
    sub = lax.broadcasted_iota(jnp.int32, (8, 512), 0)
    edge = jnp.where(first_core, 3, 0)

    def far_du(both, third):
        value = jnp.where(sub == edge, both[6:7], 0.0)
        value = jnp.where(sub == edge + 1, both[7:8], value)
        return jnp.where(sub == edge + 2, third, value)

    def rows_far(first_tile):
        return [tile(far_ref, first_tile + j) for j in range(6)]

    c_tiles, d_tiles = rows_far(10), rows_far(16)
    above = [jnp.where(even, d, c) for c, d in zip(c_tiles, d_tiles)]
    below = [jnp.where(even, c, d) for c, d in zip(c_tiles, d_tiles)]
    middle = [tile(far_ref, j) for j in range(8)]
    thirds = tile(far_ref, 8)
    x_far = jnp.concatenate(above + middle + below, axis=0)
    du_far = [far_du(above[j], above[j + 3][6:7]) for j in range(3)]
    du_far += [far_du(middle[j], thirds[j : j + 1]) for j in range(8)]
    du_far += [far_du(below[j], below[j + 3][6:7]) for j in range(3)]
    normed_far = normalize(x_far, scale)
    normed = normed_far.astype(BF16)
    raw = mm(normed, win_ref[:, 512:1024]).astype(BF16).astype(F32)
    kf_s[...] = unit(raw, ones).astype(BF16)
    vf_s[...] = mm(normed, win_ref[:, 1024:1536]).astype(BF16)
    raw = mm(normed_far[24:136].astype(BF16), win_ref[:, 0:512]).astype(BF16).astype(F32)
    qf_s[...] = (unit(raw, ones) * gain).astype(BF16)
    dof_s[...] = mm_nt(jnp.concatenate(du_far, axis=0).astype(BF16), wo_ref[...]).astype(BF16)

    mate_base = jnp.where(first_core, 16, -8)
    far_base = jnp.where(first_core, -6, 16)

    def places(index, near):
        in_near = index < near
        pair = jnp.where(in_near, index // NEAR, 0)
        j = jnp.where(in_near, index % NEAR, index - near)
        mine = in_near & (j < 32)
        eights = jnp.where(in_near, j - 32, j)
        row = jnp.where(mine, 2 * pair + j // 16, 2 * pair + eights // 8)
        slot = eights % 8
        far_col = jnp.where(slot < 6, far_base + slot, 1000)
        return row, jnp.where(mine, j % 16, jnp.where(in_near, mate_base + slot, far_col))

    key_row, key_col = places(lax.broadcasted_iota(jnp.int32, (256, 128), 0), 4 * NEAR)
    query_row, query_col = places(lax.broadcasted_iota(jnp.int32, (256, 128), 1) % 64, NEAR)
    row_gap, col_gap = key_row - query_row, key_col - query_col
    near = (row_gap >= 0) & (row_gap <= 6) & (col_gap >= -3) & (col_gap <= 3) & (key_col < 1000)
    image_col = key_col + 16 * my_col
    near = near & (image_col >= 0) & (image_col < 16 * lax.axis_size("cols"))
    bias_near = jnp.where(near, 0.0, -1e30)

    dk_s[...] = jnp.zeros_like(dk_s)
    dv_s[...] = jnp.zeros_like(dv_s)
    for i in range(7):
        image_row = key_row + (8 * my_row - 6 + 2 * i)
        inside = (image_row >= 0) & (image_row < 8 * lax.axis_size("rows"))
        bias = jnp.where(inside, bias_near, -1e30)
        bias = jnp.concatenate([bias, bias], axis=1)
        blocks = range(max(i, 3), min(i + 4, 7))
        there = slice(32 * (blocks[0] - 3), 32 * (blocks[-1] - 2))

        def own_keys(value):
            parts = [value[NEAR * (b - i) : NEAR * (b - i) + 32] for b in blocks]
            return jnp.concatenate(parts, axis=0)

        for g in range(2):
            lanes = slice(256 * g, 256 * g + 256)

            def keys(near_ref, far_ref):
                parts = [near_ref[NEAR * i : NEAR * (i + 4), lanes], far_ref[FAR * i : FAR * (i + 4), lanes]]
                return jnp.concatenate(parts, axis=0)

            def queries(near_ref, far_ref):
                parts = [near_ref[NEAR * i : NEAR * (i + 1), lanes], far_ref[FAR * i : FAR * (i + 1), lanes]]
                return by_head(jnp.concatenate(parts, axis=0))

            k_t, v_t = keys(kn_ref, kf_s), keys(vn_ref, vf_s)
            q_h, do_h = queries(qn_ref, qf_s), queries(don_ref, dof_s)
            scores = mm_nt(k_t, q_h) + bias
            weight = jnp.exp(scores - jnp.max(scores, axis=0, keepdims=True))
            weight = weight * (1.0 / jnp.sum(weight, axis=0, keepdims=True))
            prob = weight.astype(BF16)
            dprob = mm_nt(v_t, do_h).astype(BF16).astype(F32)
            mean = jnp.sum(weight * dprob, axis=0, keepdims=True)
            dscore = (weight * (dprob - mean)).astype(BF16)
            dv_s[there, lanes] += mm(own_keys(prob), do_h)
            dk_s[there, lanes] += mm(own_keys(dscore), q_h)
            if 1 <= i <= 5:
                att = own_heads(mm_tn(prob, v_t)).astype(BF16)
                dq = own_heads(mm_tn(dscore, k_t)).astype(BF16)
                for n in range(2):
                    at = 2 * i + n - 3
                    if 0 <= at < 8:
                        att_s[16 * at : 16 * at + 16, lanes] = att[16 * n : 16 * n + 16]
                        dq_s[16 * at : 16 * at + 16, lanes] = dq[16 * n : 16 * n + 16]

    att = att_s[...]
    normed = normed_ref[...]
    x = own_ref[0:128, :].astype(F32)
    out_ref[...] = (x + mm(att, wo_ref[...])).astype(BF16)

    def norm_back(raw, grad):
        inv = lax.rsqrt(head_sums(raw * raw, ones) + 1e-06)
        return inv * (grad - raw * (inv * inv) * head_sums(raw * grad, ones))

    dq = norm_back(qraw_ref[...].astype(F32), dq_s[...].astype(F32) * gain)
    dk = norm_back(kraw_ref[...].astype(F32), dk_s[...])
    gp_s[:, 0:512] = dq.astype(BF16)
    gp_s[:, 512:1024] = dk.astype(BF16)
    gp_s[:, 1024:1536] = dv_s[...].astype(BF16)
    dnormed = mm_nt(gp_s[...], win_ref[...]) * scale
    r = lax.rsqrt(jnp.mean(x * x, axis=-1, keepdims=True) + 1e-06)
    along = jnp.mean(dnormed * x, axis=-1, keepdims=True)
    dx = r * dnormed - x * (r * r * r * along)
    dx_ref[...] = (own_ref[128:256, :].astype(F32) + dx).astype(BF16)

    features_ref[0:512, :] = jnp.transpose(normed)
    features_ref[512:1024, :] = jnp.transpose(att)
    for core in range(2):

        @pl.when(my_col % 2 == core)
        def _():
            for ref, half in ((keep_ref, core), (send_ref, 1 - core)):
                ref[:, 0:768] = gp_s[:, 768 * half : 768 * half + 768]
                ref[:, 768:1024] = own_ref[128:256, 256 * half : 256 * half + 256]


def grads_kernel(factor, features_ref, keep_ref, got_features_ref, got_ref, out_ref):
    features = jnp.concatenate([features_ref[...], got_features_ref[...]], axis=1)
    grads = jnp.concatenate([keep_ref[...], got_ref[...]], axis=0)
    out_ref[:, 0:768] = (mm(features[:512], grads[:, :768]) * factor).astype(BF16)
    out_ref[:, 768:1024] = (mm(features[512:], grads[:, 768:]) * factor).astype(BF16)


def sum_kernel(rows, parts_ref, out_ref):
    count = parts_ref.shape[0] // rows
    step = max(rows, 16)
    total = parts_ref[0:step, :].astype(F32)
    for i in range(1, count * rows // step):
        total = total + parts_ref[step * i : step * (i + 1), :].astype(F32)
    while total.shape[0] > rows:
        half = total.shape[0] // 2
        total = total[:half] + total[half:]
    block = jnp.concatenate([total] * (step // rows), axis=0).astype(BF16)
    for i in range(count * rows // step):
        out_ref[step * i : step * (i + 1), :] = block


def final_kernel(half_ref, half_grads_ref, *refs):
    qkv_ref, out_ref = refs[-2:]
    qkv_ref[...] = half_grads_ref[:, 0:768].astype(F32)
    out_ref[...] = half_grads_ref[:, 768:1024].astype(F32)


def write_half(half, half_grads, *whole):
    steps = 4
    rows = half_grads.shape[0] // steps
    return pl.pallas_call(
        final_kernel,
        grid_spec=pltpu.PrefetchScalarGridSpec(
            num_scalar_prefetch=1,
            grid=(steps,),
            in_specs=[pl.BlockSpec((rows, 1024), lambda i, half: (i, 0))]
            + [pl.BlockSpec(memory_space=pl.ANY)] * len(whole),
            out_specs=[
                pl.BlockSpec((rows, 768), lambda i, half: (i, half[0])),
                pl.BlockSpec((rows, 256), lambda i, half: (i, half[0])),
            ],
        ),
        out_shape=[
            jax.ShapeDtypeStruct((512, 1536), F32),
            jax.ShapeDtypeStruct((512, 512), F32),
        ],
        input_output_aliases={2: 0, 3: 1} if whole else {},
        compiler_params=pltpu.CompilerParams(vmem_limit_bytes=8 * 1024 * 1024),
        cost_estimate=pl.CostEstimate(flops=1 << 20, bytes_accessed=3 << 20, transcendentals=0),
    )(half, half_grads, *whole)


def call(kernel, outs, scratch=(), flops=0, scalars=0, inputs=0, limit=VMEM_LIMIT):
    whole = pl.BlockSpec(memory_space=pltpu.VMEM)
    return pl.pallas_call(
        kernel,
        out_shape=outs,
        in_specs=[pl.BlockSpec(memory_space=pltpu.SMEM)] * scalars
        + [whole] * inputs,
        out_specs=jax.tree.map(lambda _: whole, outs),
        scratch_shapes=list(scratch),
        compiler_params=pltpu.CompilerParams(vmem_limit_bytes=limit),
        cost_estimate=pl.CostEstimate(flops=flops, bytes_accessed=4 << 20, transcendentals=0),
    )


def condition(noise_level_step, label, category_gain_offset, noise_level_gain_matrix):
    half_freqs = noise_level_gain_matrix.shape[0] // 2
    steps_idx = jnp.arange(half_freqs, dtype=F32)
    freq_rates = 2.0 * math.pi * jnp.exp(steps_idx * (math.log(64.0) / half_freqs))
    angles = noise_level_step[0].astype(F32) * 0.001 * freq_rates
    features = jnp.concatenate([jnp.cos(angles), jnp.sin(angles)]).astype(BF16)
    shifted = jnp.dot(features[None, :], noise_level_gain_matrix, preferred_element_type=F32)
    class_row = lax.dynamic_slice_in_dim(category_gain_offset, label[0], 1, 0).astype(F32)
    return 1.0 + class_row + shifted


def swapped(value, row_to, col_to):
    n_rows, n_cols = lax.axis_size("rows"), lax.axis_size("cols")
    pairs = []
    for r in range(n_rows):
        for c in range(n_cols):
            to_row, to_col = row_to(r), col_to(c)
            if 0 <= to_row < n_rows and 0 <= to_col < n_cols:
                pairs.append((r * n_cols + c, to_row * n_cols + to_col))
    return lax.ppermute(value, AXES, pairs)


def same(i):
    return i


def paired(i):
    return i ^ 1


def across(i):
    return i - 1 if i % 2 == 0 else i + 1


def per_device(
    grid_token_states, upstream_gradient, noise_level_step, picture_category_label,
    category_gain_offset, noise_level_gain_matrix, attention_input_matrix,
    final_projection_matrix, cosine_logit_gain,
):
    x, du = grid_token_states, upstream_gradient
    height, columns, width = x.shape
    n_rows, n_cols = lax.axis_size("rows"), lax.axis_size("cols")
    tokens = height * columns
    bf = lambda *shape: jax.ShapeDtypeStruct(shape, BF16)
    vm = pltpu.VMEM
    x2, du2 = x.reshape(tokens, width), du.reshape(tokens, width)

    to_c, to_d, own = call(
        rows_kernel, (bf(144, width), bf(144, width), bf(256, width)), inputs=2, limit=SMALL_LIMIT
    )(x2, du2)
    from_c = swapped(to_c, paired, same)
    from_d = swapped(to_d, across, same)
    mate = swapped(own, same, paired)
    scale = condition(
        noise_level_step, picture_category_label, category_gain_offset, noise_level_gain_matrix
    )
    half = (lax.axis_index("cols") % 2).astype(jnp.int32).reshape(1)
    to_far, to_mate = call(
        columns_kernel, (bf(176, width), bf(288, width)), flops=16 << 30, inputs=3, limit=SMALL_LIMIT
    )(own, from_c, from_d)
    far = swapped(to_far, same, across)
    mate_rows = swapped(to_mate, same, paired)
    weights = (attention_input_matrix, final_projection_matrix, scale)
    k, v, q, do, kraw, qraw, normed = call(
        near_kernel,
        (bf(480, width), bf(480, width), bf(336, width), bf(336, width), bf(128, width), bf(128, width), bf(128, width)),
        scratch=[vm((320, 512), F32), vm((160, 512), F32), vm((336, 512), BF16)],
        flops=4 << 30, scalars=1, inputs=8,
    )(cosine_logit_gain, own, mate, from_c, from_d, mate_rows, *weights)

    output, grad_latent, features, send, keep = call(
        main_kernel,
        (bf(tokens, width), bf(tokens, width), bf(1024, tokens), bf(tokens, 1024), bf(tokens, 1024)),
        scratch=[
            vm((160, 512), BF16), vm((160, 512), BF16), vm((112, 512), BF16), vm((112, 512), BF16),
            vm((128, 512), BF16), vm((128, 512), BF16), vm((128, 512), F32), vm((128, 512), F32),
            vm((128, 1536), BF16),
        ],
        flops=8 << 30, scalars=1, inputs=12,
    )(cosine_logit_gain, own, far, k, v, q, do, kraw, qraw, normed, *weights)

    got_features = swapped(features, same, paired)
    got = swapped(send, same, paired)
    factor = 1.0 / math.sqrt(tokens * n_rows * n_cols)
    partial = call(
        functools.partial(grads_kernel, factor), bf(512, 1024), flops=1 << 29, inputs=4, limit=SMALL_LIMIT
    )(features, keep, got_features, got)

    groups = [
        [r * n_cols + 2 * c + core_ for r in range(n_rows) for c in range(n_cols // 2)]
        for core_ in range(2)
    ]
    members = n_rows * n_cols // 2
    each = 512 // members

    def exchange(value):
        return lax.all_to_all(
            value.reshape(members, each, 1024), AXES, 0, 0, axis_index_groups=groups, tiled=True
        ).reshape(512, 1024)

    summed = call(
        functools.partial(sum_kernel, each), bf(512, 1024), inputs=1, limit=SMALL_LIMIT
    )(exchange(partial))
    mine = exchange(summed)
    other = swapped(mine, same, paired)
    qkv_grad, out_grad = write_half(1 - half, other, *write_half(half, mine))
    return output.reshape(x.shape), grad_latent.reshape(x.shape), qkv_grad, out_grad


def solution(mesh):
    placed = (P("rows", "cols", None), P("rows", "cols", None)) + (P(),) * 7
    return jax.shard_map(
        per_device,
        mesh=mesh,
        in_specs=placed,
        out_specs=(P("rows", "cols", None), P("rows", "cols", None), P(), P()),
        check_vma=False,
    )
```

```python
import functools
import math

import jax
import jax.numpy as jnp
from jax import lax
from jax.experimental import pallas as pl
from jax.experimental.pallas import tpu as pltpu
from jax.sharding import PartitionSpec as P

HEADS = 8
HEAD = 64
BF16 = jnp.bfloat16
F32 = jnp.float32
VMEM_LIMIT = 28 * 1024 * 1024
SMALL_LIMIT = 8 * 1024 * 1024
AXES = ("rows", "cols")
NEAR, FAR = 48, 16


def mm(a, b):
    return jnp.dot(a, b, preferred_element_type=F32)


def mm_nt(a, b):
    return lax.dot_general(a, b, (((1,), (1,)), ((), ())), preferred_element_type=F32)


def mm_tn(a, b):
    return lax.dot_general(a, b, (((0,), (0,)), ((), ())), preferred_element_type=F32)


def head_sums(product, ones):
    high = product.astype(BF16)
    low = (product - high.astype(F32)).astype(BF16)
    parts = []
    for g in range(2):
        lanes = slice(256 * g, 256 * g + 256)
        parts.append(mm(high[:, lanes], ones) + mm(low[:, lanes], ones))
    return jnp.concatenate(parts, axis=1)


def by_head(block):
    head_of = lax.broadcasted_iota(jnp.int32, block.shape, 1) // HEAD
    zero = jnp.zeros_like(block)
    return jnp.concatenate([jnp.where(head_of == h, block, zero) for h in range(4)], axis=0)


def own_heads(result):
    head_of = lax.broadcasted_iota(jnp.int32, (32, 256), 1) // HEAD
    total = result[:32]
    for h in range(1, 4):
        total = jnp.where(head_of == h, result[HEAD * h : HEAD * h + 32], total)
    return total


def head_ones():
    row_head = lax.broadcasted_iota(jnp.int32, (256, 256), 0) // HEAD
    lane_head = lax.broadcasted_iota(jnp.int32, (256, 256), 1) // HEAD
    return jnp.where(row_head == lane_head, 1.0, 0.0).astype(BF16)


def lane_gain(gain_ref):
    head_of = lax.broadcasted_iota(jnp.int32, (1, 512), 1) // HEAD
    gain = jnp.zeros((1, 512), F32)
    for h in range(HEADS):
        gain = jnp.where(head_of == h, gain_ref[h], gain)
    return gain


def block(ref, index):
    return ref[16 * index : 16 * index + 16, :].astype(F32)


def tile(ref, index):
    return block(ref, index // 2)[8 * (index % 2) : 8 * (index % 2) + 8]


def normalize(x, scale):
    return x * lax.rsqrt(jnp.mean(x * x, axis=-1, keepdims=True) + 1e-06) * scale


def unit(raw, ones):
    return raw * lax.rsqrt(head_sums(raw * raw, ones) + 1e-06)


def rows_kernel(x_ref, du_ref, c_ref, d_ref, own_ref):
    even = lax.axis_index("rows") % 2 == 0
    own_ref[0:128, :] = x_ref[...]
    own_ref[128:256, :] = du_ref[...]
    for ref, take_last in ((c_ref, even), (d_ref, jnp.logical_not(even))):

        @pl.when(take_last)
        def _():
            ref[0:96, :] = x_ref[32:128, :]
            ref[96:144, :] = du_ref[80:128, :]

        @pl.when(jnp.logical_not(take_last))
        def _():
            ref[0:96, :] = x_ref[0:96, :]
            ref[96:144, :] = du_ref[0:48, :]


def columns_kernel(own_ref, c_ref, d_ref, _scale, _row, _bias, far_ref, both_ref):
    even = lax.axis_index("rows") % 2 == 0
    first_core = lax.axis_index("cols") % 2 == 0
    sub = lax.broadcasted_iota(jnp.int32, (8, 512), 0)
    both_ref[0:144, :] = c_ref[...]
    both_ref[144:288, :] = d_ref[...]

    def x_edge(x):
        return jnp.where(first_core, x, pltpu.roll(x, 6, 0))[:8]

    def du_edge(du):
        third = jnp.where(first_core, du[2:3], du[15:16])
        return jnp.where(first_core, pltpu.roll(du, 6, 0), pltpu.roll(du, 9, 0))[:8], third

    tiles = []
    thirds = jnp.zeros((8, 512), F32)
    for row in range(8):
        two, third = du_edge(block(own_ref, 8 + row))
        tiles.append(jnp.where(sub < 6, x_edge(block(own_ref, row)), two))
        thirds = jnp.where(sub == row, third, thirds)
    tiles += [thirds, jnp.zeros((8, 512), F32)]
    for ref in (c_ref, d_ref):
        edges = [du_edge(block(ref, 6 + j)) for j in range(3)]
        for j in range(6):
            rest = edges[j][0] if j < 3 else edges[j - 3][1]
            tiles.append(jnp.where(sub < 6, x_edge(block(ref, j)), rest))
    for i in range(11):
        far_ref[16 * i : 16 * i + 16, :] = jnp.concatenate(tiles[2 * i : 2 * i + 2], 0).astype(BF16)


def near_kernel(
    gain_ref, own_ref, mate_ref, rows_ref, mate_rows_ref, win_ref, wo_ref, scale_ref,
    k_ref, v_ref, q_ref, do_ref, kraw_ref, qraw_ref, normed_ref,
    own_s, mate_s, du_s,
):
    even = lax.axis_index("rows") % 2 == 0
    first_core = lax.axis_index("cols") % 2 == 0
    scale = scale_ref[...]
    gain = lane_gain(gain_ref)
    ones = head_ones()

    def pick(low, high, above):
        return jnp.where(even, high, low) if above else jnp.where(even, low, high)

    def row_parts(row, first):
        if 0 <= row < 8:
            own, mate = block(own_ref, first + row), block(mate_ref, first + row)
        else:
            above = row < 0
            j = (row + (6 if above else -8)) if first == 0 else 6 + (row + (3 if above else -8))
            own = pick(block(rows_ref, j), block(rows_ref, 9 + j), above)
            mate = pick(block(mate_rows_ref, j), block(mate_rows_ref, 9 + j), above)
        return own, jnp.where(first_core, mate[:8], mate[8:])

    for e in range(20):
        own, mate = row_parts(e - 6, 0)
        own_s[16 * e : 16 * e + 16, :] = normalize(own, scale)
        mate_s[8 * e : 8 * e + 8, :] = normalize(mate, scale)
    normed_ref[...] = own_s[96:224, :].astype(BF16)
    for i in range(7):
        first, second = row_parts(2 * i - 3, 8), row_parts(2 * i - 2, 8)
        pair = jnp.concatenate([first[0], second[0], first[1], second[1]], axis=0)
        du_s[NEAR * i : NEAR * (i + 1), :] = pair.astype(BF16)

    def normed_pairs(first_row, count):
        parts = []
        for n in range(count):
            row = first_row + 2 * n
            parts += [own_s[16 * row : 16 * row + 32, :], mate_s[8 * row : 8 * row + 16, :]]
        return jnp.concatenate(parts, axis=0).astype(BF16)

    for t in range(5):
        rows = slice(96 * t, 96 * t + 96)
        normed = normed_pairs(4 * t, 2)
        raw = mm(normed, win_ref[:, 512:1024]).astype(BF16).astype(F32)
        k_ref[rows, :] = unit(raw, ones).astype(BF16)
        v_ref[rows, :] = mm(normed, win_ref[:, 1024:1536]).astype(BF16)
        for n in range(2):
            at = 2 * t + n - 3
            if 0 <= at < 4:
                kraw_ref[32 * at : 32 * at + 32, :] = raw[48 * n : 48 * n + 32].astype(BF16)
    for first, count in ((0, 2), (2, 2), (4, 2), (6, 1)):
        rows = slice(NEAR * first, NEAR * (first + count))
        normed = normed_pairs(3 + 2 * first, count)
        raw = mm(normed, win_ref[:, 0:512]).astype(BF16).astype(F32)
        q_ref[rows, :] = (unit(raw, ones) * gain).astype(BF16)
        do_ref[rows, :] = mm_nt(du_s[rows, :], wo_ref[...]).astype(BF16)
        for n in range(2 * count):
            at = 2 * first + n - 3
            if 0 <= at < 8:
                here = 48 * (n // 2) + 16 * (n % 2)
                qraw_ref[16 * at : 16 * at + 16, :] = raw[here : here + 16].astype(BF16)


def mask_kernel(row_ref, bias_ref):
    my_col = lax.axis_index("cols")
    first_core = my_col % 2 == 0
    mate_base = jnp.where(first_core, 16, -8)
    far_base = jnp.where(first_core, -6, 16)

    def places(index, near):
        in_near = index < near
        pair = jnp.where(in_near, index // NEAR, 0)
        j = jnp.where(in_near, index % NEAR, index - near)
        mine = in_near & (j < 32)
        eights = jnp.where(in_near, j - 32, j)
        row = jnp.where(mine, 2 * pair + j // 16, 2 * pair + eights // 8)
        slot = eights % 8
        far_col = jnp.where(slot < 6, far_base + slot, 1000)
        return row, jnp.where(mine, j % 16, jnp.where(in_near, mate_base + slot, far_col))

    key_row, key_col = places(lax.broadcasted_iota(jnp.int32, (256, 128), 0), 4 * NEAR)
    query_row, query_col = places(lax.broadcasted_iota(jnp.int32, (256, 128), 1) % 64, NEAR)
    row_gap, col_gap = key_row - query_row, key_col - query_col
    near = (row_gap >= 0) & (row_gap <= 6) & (col_gap >= -3) & (col_gap <= 3) & (key_col < 1000)
    image_col = key_col + 16 * my_col
    near = near & (image_col >= 0) & (image_col < 16 * lax.axis_size("cols"))
    row_ref[...] = key_row
    bias_ref[...] = jnp.where(near, 0.0, -1e30)


def main_kernel(
    gain_ref, own_ref, far_ref, kn_ref, vn_ref, qn_ref, don_ref, kraw_ref, qraw_ref, normed_ref,
    row_ref, bias_ref, win_ref, wo_ref, scale_ref,
    out_ref, dx_ref, features_ref, send_ref, keep_ref,
    kf_s, vf_s, qf_s, dof_s, att_s, dq_s, dk_s, dv_s, gp_s,
):
    my_row, my_col = lax.axis_index("rows"), lax.axis_index("cols")
    even = my_row % 2 == 0
    first_core = my_col % 2 == 0
    scale = scale_ref[...]
    gain = lane_gain(gain_ref)
    ones = head_ones()
    sub = lax.broadcasted_iota(jnp.int32, (8, 512), 0)
    edge = jnp.where(first_core, 3, 0)

    def far_du(both, third):
        value = jnp.where(sub == edge, both[6:7], 0.0)
        value = jnp.where(sub == edge + 1, both[7:8], value)
        return jnp.where(sub == edge + 2, third, value)

    def rows_far(first_tile):
        return [tile(far_ref, first_tile + j) for j in range(6)]

    c_tiles, d_tiles = rows_far(10), rows_far(16)
    above = [jnp.where(even, d, c) for c, d in zip(c_tiles, d_tiles)]
    below = [jnp.where(even, c, d) for c, d in zip(c_tiles, d_tiles)]
    middle = [tile(far_ref, j) for j in range(8)]
    thirds = tile(far_ref, 8)
    x_far = jnp.concatenate(above + middle + below, axis=0)
    du_far = [far_du(above[j], above[j + 3][6:7]) for j in range(3)]
    du_far += [far_du(middle[j], thirds[j : j + 1]) for j in range(8)]
    du_far += [far_du(below[j], below[j + 3][6:7]) for j in range(3)]
    normed_far = normalize(x_far, scale)
    normed = normed_far.astype(BF16)
    raw = mm(normed, win_ref[:, 512:1024]).astype(BF16).astype(F32)
    kf_s[...] = unit(raw, ones).astype(BF16)
    vf_s[...] = mm(normed, win_ref[:, 1024:1536]).astype(BF16)
    raw = mm(normed_far[24:136].astype(BF16), win_ref[:, 0:512]).astype(BF16).astype(F32)
    qf_s[...] = (unit(raw, ones) * gain).astype(BF16)
    dof_s[...] = mm_nt(jnp.concatenate(du_far, axis=0).astype(BF16), wo_ref[...]).astype(BF16)

    dk_s[...] = jnp.zeros_like(dk_s)
    dv_s[...] = jnp.zeros_like(dv_s)
    for i in range(7):
        image_row = row_ref[...] + (8 * my_row - 6 + 2 * i)
        inside = (image_row >= 0) & (image_row < 8 * lax.axis_size("rows"))
        bias = jnp.where(inside, bias_ref[...], -1e30)
        bias = jnp.concatenate([bias, bias], axis=1)
        blocks = range(max(i, 3), min(i + 4, 7))
        there = slice(32 * (blocks[0] - 3), 32 * (blocks[-1] - 2))

        def own_keys(value):
            parts = [value[NEAR * (b - i) : NEAR * (b - i) + 32] for b in blocks]
            return jnp.concatenate(parts, axis=0)

        for g in range(2):
            lanes = slice(256 * g, 256 * g + 256)

            def keys(near_ref, far_ref):
                parts = [near_ref[NEAR * i : NEAR * (i + 4), lanes], far_ref[FAR * i : FAR * (i + 4), lanes]]
                return jnp.concatenate(parts, axis=0)

            def queries(near_ref, far_ref):
                parts = [near_ref[NEAR * i : NEAR * (i + 1), lanes], far_ref[FAR * i : FAR * (i + 1), lanes]]
                return by_head(jnp.concatenate(parts, axis=0))

            k_t, v_t = keys(kn_ref, kf_s), keys(vn_ref, vf_s)
            q_h, do_h = queries(qn_ref, qf_s), queries(don_ref, dof_s)
            scores = mm_nt(k_t, q_h) + bias
            weight = jnp.exp(scores - jnp.max(scores, axis=0, keepdims=True))
            weight = weight * (1.0 / jnp.sum(weight, axis=0, keepdims=True))
            prob = weight.astype(BF16)
            dprob = mm_nt(v_t, do_h)
            mean = jnp.sum(weight * dprob, axis=0, keepdims=True)
            dscore = (weight * (dprob - mean)).astype(BF16)
            dv_s[there, lanes] += mm(own_keys(prob), do_h)
            dk_s[there, lanes] += mm(own_keys(dscore), q_h)
            if 1 <= i <= 5:
                att = own_heads(mm_tn(prob, v_t)).astype(BF16)
                dq = own_heads(mm_tn(dscore, k_t)).astype(BF16)
                for n in range(2):
                    at = 2 * i + n - 3
                    if 0 <= at < 8:
                        att_s[16 * at : 16 * at + 16, lanes] = att[16 * n : 16 * n + 16]
                        dq_s[16 * at : 16 * at + 16, lanes] = dq[16 * n : 16 * n + 16]

    att = att_s[...]
    normed = normed_ref[...]
    x = own_ref[0:128, :].astype(F32)
    out_ref[...] = (x + mm(att, wo_ref[...])).astype(BF16)

    def norm_back(raw, grad):
        inv = lax.rsqrt(head_sums(raw * raw, ones) + 1e-06)
        return inv * (grad - raw * (inv * inv) * head_sums(raw * grad, ones))

    dq = norm_back(qraw_ref[...].astype(F32), dq_s[...].astype(F32) * gain)
    dk = norm_back(kraw_ref[...].astype(F32), dk_s[...])
    gp_s[:, 0:512] = dq.astype(BF16)
    gp_s[:, 512:1024] = dk.astype(BF16)
    gp_s[:, 1024:1536] = dv_s[...].astype(BF16)
    dnormed = mm_nt(gp_s[...], win_ref[...]) * scale
    r = lax.rsqrt(jnp.mean(x * x, axis=-1, keepdims=True) + 1e-06)
    along = jnp.mean(dnormed * x, axis=-1, keepdims=True)
    dx = r * dnormed - x * (r * r * r * along)
    dx_ref[...] = (own_ref[128:256, :].astype(F32) + dx).astype(BF16)

    features_ref[0:512, :] = jnp.transpose(normed)
    features_ref[512:1024, :] = jnp.transpose(att)
    for core in range(2):

        @pl.when(my_col % 2 == core)
        def _():
            for ref, half in ((keep_ref, core), (send_ref, 1 - core)):
                ref[:, 0:768] = gp_s[:, 768 * half : 768 * half + 768]
                ref[:, 768:1024] = own_ref[128:256, 256 * half : 256 * half + 256]


def grads_kernel(factor, features_ref, keep_ref, got_features_ref, got_ref, out_ref):
    features = jnp.concatenate([features_ref[...], got_features_ref[...]], axis=1)
    grads = jnp.concatenate([keep_ref[...], got_ref[...]], axis=0)
    out_ref[:, 0:768] = (mm(features[:512], grads[:, :768]) * factor).astype(BF16)
    out_ref[:, 768:1024] = (mm(features[512:], grads[:, 768:]) * factor).astype(BF16)


def sum_kernel(rows, parts_ref, out_ref):
    count = parts_ref.shape[0] // rows
    step = max(rows, 16)
    total = parts_ref[0:step, :].astype(F32)
    for i in range(1, count * rows // step):
        total = total + parts_ref[step * i : step * (i + 1), :].astype(F32)
    while total.shape[0] > rows:
        half = total.shape[0] // 2
        total = total[:half] + total[half:]
    block = jnp.concatenate([total] * (step // rows), axis=0).astype(BF16)
    for i in range(count * rows // step):
        out_ref[step * i : step * (i + 1), :] = block


def final_kernel(mine, grads_ref, *refs):
    qkv_ref, out_ref, qkv_s, out_s, sems = refs[-5:]
    steps = sems.shape[1]
    rows = grads_ref.shape[0] // steps
    for core in range(2):

        @pl.when(lax.axis_index("cols") % 2 == core)
        def _():
            half = core if mine else 1 - core
            copies = []
            for i in range(steps):
                part = slice(rows * i, rows * (i + 1))
                qkv_s[part, :] = grads_ref[part, 0:768].astype(F32)
                out_s[part, :] = grads_ref[part, 768:1024].astype(F32)
                lanes = slice(768 * half, 768 * half + 768)
                copies.append(pltpu.make_async_copy(qkv_s.at[part], qkv_ref.at[part, lanes], sems.at[0, i]))
                lanes = slice(256 * half, 256 * half + 256)
                copies.append(pltpu.make_async_copy(out_s.at[part], out_ref.at[part, lanes], sems.at[1, i]))
                copies[-2].start()
                copies[-1].start()
            for copy in copies:
                copy.wait()


def write_half(mine, half_grads, *whole):
    unplaced = pl.BlockSpec(memory_space=pl.ANY)
    return pl.pallas_call(
        functools.partial(final_kernel, mine),
        in_specs=[pl.BlockSpec(memory_space=pltpu.VMEM)] + [unplaced] * len(whole),
        out_specs=[unplaced, unplaced],
        out_shape=[
            jax.ShapeDtypeStruct((512, 1536), F32),
            jax.ShapeDtypeStruct((512, 512), F32),
        ],
        scratch_shapes=[
            pltpu.VMEM((512, 768), F32), pltpu.VMEM((512, 256), F32), pltpu.SemaphoreType.DMA((2, 8)),
        ],
        input_output_aliases={1: 0, 2: 1} if whole else {},
        compiler_params=pltpu.CompilerParams(vmem_limit_bytes=SMALL_LIMIT),
        cost_estimate=pl.CostEstimate(flops=1 << 20, bytes_accessed=3 << 20, transcendentals=0),
    )(half_grads, *whole)


def call(kernel, outs, scratch=(), flops=0, scalars=0, inputs=0, limit=VMEM_LIMIT):
    whole = pl.BlockSpec(memory_space=pltpu.VMEM)
    return pl.pallas_call(
        kernel,
        out_shape=outs,
        in_specs=[pl.BlockSpec(memory_space=pltpu.SMEM)] * scalars
        + [whole] * inputs,
        out_specs=jax.tree.map(lambda _: whole, outs),
        scratch_shapes=list(scratch),
        compiler_params=pltpu.CompilerParams(vmem_limit_bytes=limit),
        cost_estimate=pl.CostEstimate(flops=flops, bytes_accessed=4 << 20, transcendentals=0),
    )


def condition(noise_level_step, label, category_gain_offset, noise_level_gain_matrix):
    half_freqs = noise_level_gain_matrix.shape[0] // 2
    steps_idx = jnp.arange(half_freqs, dtype=F32)
    freq_rates = 2.0 * math.pi * jnp.exp(steps_idx * (math.log(64.0) / half_freqs))
    angles = noise_level_step[0].astype(F32) * 0.001 * freq_rates
    features = jnp.concatenate([jnp.cos(angles), jnp.sin(angles)]).astype(BF16)
    shifted = jnp.dot(features[None, :], noise_level_gain_matrix, preferred_element_type=F32)
    class_row = lax.dynamic_slice_in_dim(category_gain_offset, label[0], 1, 0).astype(F32)
    return 1.0 + class_row + shifted


def swapped(value, row_to, col_to):
    n_rows, n_cols = lax.axis_size("rows"), lax.axis_size("cols")
    pairs = []
    for r in range(n_rows):
        for c in range(n_cols):
            to_row, to_col = row_to(r), col_to(c)
            if 0 <= to_row < n_rows and 0 <= to_col < n_cols:
                pairs.append((r * n_cols + c, to_row * n_cols + to_col))
    return lax.ppermute(value, AXES, pairs)


def same(i):
    return i


def paired(i):
    return i ^ 1


def across(i):
    return i - 1 if i % 2 == 0 else i + 1


def per_device(
    grid_token_states, upstream_gradient, noise_level_step, picture_category_label,
    category_gain_offset, noise_level_gain_matrix, attention_input_matrix,
    final_projection_matrix, cosine_logit_gain,
):
    x, du = grid_token_states, upstream_gradient
    height, columns, width = x.shape
    n_rows, n_cols = lax.axis_size("rows"), lax.axis_size("cols")
    tokens = height * columns
    bf = lambda *shape: jax.ShapeDtypeStruct(shape, BF16)
    vm = pltpu.VMEM
    x2, du2 = x.reshape(tokens, width), du.reshape(tokens, width)

    to_c, to_d, own = call(
        rows_kernel, (bf(144, width), bf(144, width), bf(256, width)), inputs=2, limit=SMALL_LIMIT
    )(x2, du2)
    from_c = swapped(to_c, paired, same)
    from_d = swapped(to_d, across, same)
    mate = swapped(own, same, paired)
    scale = condition(
        noise_level_step, picture_category_label, category_gain_offset, noise_level_gain_matrix
    )
    mask = call(
        mask_kernel,
        (jax.ShapeDtypeStruct((256, 128), jnp.int32), jax.ShapeDtypeStruct((256, 128), F32)),
        limit=SMALL_LIMIT,
    )()
    to_far, rows = call(
        columns_kernel, (bf(176, width), bf(288, width)), flops=16 << 30, inputs=6, limit=SMALL_LIMIT
    )(own, from_c, from_d, scale, *mask)
    far = swapped(to_far, same, across)
    mate_rows = swapped(rows, same, paired)
    weights = (attention_input_matrix, final_projection_matrix, scale)
    k, v, q, do, kraw, qraw, normed = call(
        near_kernel,
        (bf(480, width), bf(480, width), bf(336, width), bf(336, width), bf(128, width), bf(128, width), bf(128, width)),
        scratch=[vm((320, 512), F32), vm((160, 512), F32), vm((336, 512), BF16)],
        flops=4 << 30, scalars=1, inputs=7,
    )(cosine_logit_gain, own, mate, rows, mate_rows, *weights)

    output, grad_latent, features, send, keep = call(
        main_kernel,
        (bf(tokens, width), bf(tokens, width), bf(1024, tokens), bf(tokens, 1024), bf(tokens, 1024)),
        scratch=[
            vm((160, 512), BF16), vm((160, 512), BF16), vm((112, 512), BF16), vm((112, 512), BF16),
            vm((128, 512), BF16), vm((128, 512), BF16), vm((128, 512), F32), vm((128, 512), F32),
            vm((128, 1536), BF16),
        ],
        flops=8 << 30, scalars=1, inputs=14,
    )(cosine_logit_gain, own, far, k, v, q, do, kraw, qraw, normed, *mask, *weights)

    got_features = swapped(features, same, paired)
    got = swapped(send, same, paired)
    factor = 1.0 / math.sqrt(tokens * n_rows * n_cols)
    partial = call(
        functools.partial(grads_kernel, factor), bf(512, 1024), flops=1 << 29, inputs=4, limit=SMALL_LIMIT
    )(features, keep, got_features, got)

    groups = [
        [r * n_cols + 2 * c + core_ for r in range(n_rows) for c in range(n_cols // 2)]
        for core_ in range(2)
    ]
    members = n_rows * n_cols // 2
    each = 512 // members

    def exchange(value):
        return lax.all_to_all(
            value.reshape(members, each, 1024), AXES, 0, 0, axis_index_groups=groups, tiled=True
        ).reshape(512, 1024)

    summed = call(
        functools.partial(sum_kernel, each), bf(512, 1024), inputs=1, limit=SMALL_LIMIT
    )(exchange(partial))
    mine = exchange(summed)
    other = swapped(mine, same, paired)
    qkv_grad, out_grad = write_half(False, other, *write_half(True, mine))
    return output.reshape(x.shape), grad_latent.reshape(x.shape), qkv_grad, out_grad


def solution(mesh):
    placed = (P("rows", "cols", None), P("rows", "cols", None)) + (P(),) * 7
    return jax.shard_map(
        per_device,
        mesh=mesh,
        in_specs=placed,
        out_specs=(P("rows", "cols", None), P("rows", "cols", None), P(), P()),
        check_vma=False,
    )
```

```python
import functools
import math

import jax
import jax.numpy as jnp
from jax import lax
from jax.experimental import pallas as pl
from jax.experimental.pallas import tpu as pltpu
from jax.sharding import PartitionSpec as P

HEADS = 8
HEAD = 64
BF16 = jnp.bfloat16
F32 = jnp.float32
VMEM_LIMIT = 28 * 1024 * 1024
SMALL_LIMIT = 8 * 1024 * 1024
AXES = ("rows", "cols")
NEAR, FAR = 48, 16


def mm(a, b):
    return jnp.dot(a, b, preferred_element_type=F32)


def mm_nt(a, b):
    return lax.dot_general(a, b, (((1,), (1,)), ((), ())), preferred_element_type=F32)


def mm_tn(a, b):
    return lax.dot_general(a, b, (((0,), (0,)), ((), ())), preferred_element_type=F32)


def head_sums(product, ones):
    high = product.astype(BF16)
    low = (product - high.astype(F32)).astype(BF16)
    parts = []
    for g in range(2):
        lanes = slice(256 * g, 256 * g + 256)
        parts.append(mm(high[:, lanes], ones) + mm(low[:, lanes], ones))
    return jnp.concatenate(parts, axis=1)


def by_head(block):
    head_of = lax.broadcasted_iota(jnp.int32, block.shape, 1) // HEAD
    zero = jnp.zeros_like(block)
    return jnp.concatenate([jnp.where(head_of == h, block, zero) for h in range(4)], axis=0)


def own_heads(result):
    head_of = lax.broadcasted_iota(jnp.int32, (32, 256), 1) // HEAD
    total = result[:32]
    for h in range(1, 4):
        total = jnp.where(head_of == h, result[HEAD * h : HEAD * h + 32], total)
    return total


def head_ones():
    row_head = lax.broadcasted_iota(jnp.int32, (256, 256), 0) // HEAD
    lane_head = lax.broadcasted_iota(jnp.int32, (256, 256), 1) // HEAD
    return jnp.where(row_head == lane_head, 1.0, 0.0).astype(BF16)


def lane_gain(gain_ref):
    head_of = lax.broadcasted_iota(jnp.int32, (1, 512), 1) // HEAD
    gain = jnp.zeros((1, 512), F32)
    for h in range(HEADS):
        gain = jnp.where(head_of == h, gain_ref[h], gain)
    return gain


def block(ref, index):
    return ref[16 * index : 16 * index + 16, :].astype(F32)


def tile(ref, index):
    return block(ref, index // 2)[8 * (index % 2) : 8 * (index % 2) + 8]


def normalize(x, scale):
    return x * lax.rsqrt(jnp.mean(x * x, axis=-1, keepdims=True) + 1e-06) * scale


def unit(raw, ones):
    return raw * lax.rsqrt(head_sums(raw * raw, ones) + 1e-06)


def rows_kernel(own_ref, c_ref, d_ref):
    even = lax.axis_index("rows") % 2 == 0
    for ref, take_last in ((c_ref, even), (d_ref, jnp.logical_not(even))):

        @pl.when(take_last)
        def _():
            ref[0:96, :] = own_ref[32:128, :]
            ref[96:144, :] = own_ref[208:256, :]

        @pl.when(jnp.logical_not(take_last))
        def _():
            ref[0:96, :] = own_ref[0:96, :]
            ref[96:144, :] = own_ref[128:176, :]


def columns_kernel(own_ref, c_ref, d_ref, _mate, _scale, _row, _bias, far_ref, both_ref):
    even = lax.axis_index("rows") % 2 == 0
    first_core = lax.axis_index("cols") % 2 == 0
    sub = lax.broadcasted_iota(jnp.int32, (8, 512), 0)
    both_ref[0:144, :] = c_ref[...]
    both_ref[144:288, :] = d_ref[...]

    def x_edge(x):
        return jnp.where(first_core, x, pltpu.roll(x, 6, 0))[:8]

    def du_edge(du):
        third = jnp.where(first_core, du[2:3], du[15:16])
        return jnp.where(first_core, pltpu.roll(du, 6, 0), pltpu.roll(du, 9, 0))[:8], third

    tiles = []
    thirds = jnp.zeros((8, 512), F32)
    for row in range(8):
        two, third = du_edge(block(own_ref, 8 + row))
        tiles.append(jnp.where(sub < 6, x_edge(block(own_ref, row)), two))
        thirds = jnp.where(sub == row, third, thirds)
    tiles += [thirds, jnp.zeros((8, 512), F32)]
    for ref in (c_ref, d_ref):
        edges = [du_edge(block(ref, 6 + j)) for j in range(3)]
        for j in range(6):
            rest = edges[j][0] if j < 3 else edges[j - 3][1]
            tiles.append(jnp.where(sub < 6, x_edge(block(ref, j)), rest))
    for i in range(11):
        far_ref[16 * i : 16 * i + 16, :] = jnp.concatenate(tiles[2 * i : 2 * i + 2], 0).astype(BF16)


def near_kernel(
    gain_ref, own_ref, mate_ref, rows_ref, mate_rows_ref, win_ref, wo_ref, scale_ref,
    k_ref, v_ref, q_ref, do_ref, kraw_ref, qraw_ref, normed_ref,
    own_s, mate_s, du_s,
):
    even = lax.axis_index("rows") % 2 == 0
    first_core = lax.axis_index("cols") % 2 == 0
    scale = scale_ref[...]
    gain = lane_gain(gain_ref)
    ones = head_ones()

    def pick(low, high, above):
        return jnp.where(even, high, low) if above else jnp.where(even, low, high)

    def row_parts(row, first):
        if 0 <= row < 8:
            own, mate = block(own_ref, first + row), block(mate_ref, first + row)
        else:
            above = row < 0
            j = (row + (6 if above else -8)) if first == 0 else 6 + (row + (3 if above else -8))
            own = pick(block(rows_ref, j), block(rows_ref, 9 + j), above)
            mate = pick(block(mate_rows_ref, j), block(mate_rows_ref, 9 + j), above)
        return own, jnp.where(first_core, mate[:8], mate[8:])

    for e in range(20):
        own, mate = row_parts(e - 6, 0)
        own_s[16 * e : 16 * e + 16, :] = normalize(own, scale)
        mate_s[8 * e : 8 * e + 8, :] = normalize(mate, scale)
    normed_ref[...] = own_s[96:224, :].astype(BF16)
    for i in range(7):
        first, second = row_parts(2 * i - 3, 8), row_parts(2 * i - 2, 8)
        pair = jnp.concatenate([first[0], second[0], first[1], second[1]], axis=0)
        du_s[NEAR * i : NEAR * (i + 1), :] = pair.astype(BF16)

    def normed_pairs(first_row, count):
        parts = []
        for n in range(count):
            row = first_row + 2 * n
            parts += [own_s[16 * row : 16 * row + 32, :], mate_s[8 * row : 8 * row + 16, :]]
        return jnp.concatenate(parts, axis=0).astype(BF16)

    for t in range(5):
        rows = slice(96 * t, 96 * t + 96)
        normed = normed_pairs(4 * t, 2)
        raw = mm(normed, win_ref[:, 512:1024]).astype(BF16).astype(F32)
        k_ref[rows, :] = unit(raw, ones).astype(BF16)
        v_ref[rows, :] = mm(normed, win_ref[:, 1024:1536]).astype(BF16)
        for n in range(2):
            at = 2 * t + n - 3
            if 0 <= at < 4:
                kraw_ref[32 * at : 32 * at + 32, :] = raw[48 * n : 48 * n + 32].astype(BF16)
    for first, count in ((0, 2), (2, 2), (4, 2), (6, 1)):
        rows = slice(NEAR * first, NEAR * (first + count))
        normed = normed_pairs(3 + 2 * first, count)
        raw = mm(normed, win_ref[:, 0:512]).astype(BF16).astype(F32)
        q_ref[rows, :] = (unit(raw, ones) * gain).astype(BF16)
        do_ref[rows, :] = mm_nt(du_s[rows, :], wo_ref[...]).astype(BF16)
        for n in range(2 * count):
            at = 2 * first + n - 3
            if 0 <= at < 8:
                here = 48 * (n // 2) + 16 * (n % 2)
                qraw_ref[16 * at : 16 * at + 16, :] = raw[here : here + 16].astype(BF16)


def mask_kernel(row_ref, bias_ref):
    my_col = lax.axis_index("cols")
    first_core = my_col % 2 == 0
    mate_base = jnp.where(first_core, 16, -8)
    far_base = jnp.where(first_core, -6, 16)

    def places(index, near):
        in_near = index < near
        pair = jnp.where(in_near, index // NEAR, 0)
        j = jnp.where(in_near, index % NEAR, index - near)
        mine = in_near & (j < 32)
        eights = jnp.where(in_near, j - 32, j)
        row = jnp.where(mine, 2 * pair + j // 16, 2 * pair + eights // 8)
        slot = eights % 8
        far_col = jnp.where(slot < 6, far_base + slot, 1000)
        return row, jnp.where(mine, j % 16, jnp.where(in_near, mate_base + slot, far_col))

    key_row, key_col = places(lax.broadcasted_iota(jnp.int32, (256, 128), 0), 4 * NEAR)
    query_row, query_col = places(lax.broadcasted_iota(jnp.int32, (256, 128), 1) % 64, NEAR)
    row_gap, col_gap = key_row - query_row, key_col - query_col
    near = (row_gap >= 0) & (row_gap <= 6) & (col_gap >= -3) & (col_gap <= 3) & (key_col < 1000)
    image_col = key_col + 16 * my_col
    near = near & (image_col >= 0) & (image_col < 16 * lax.axis_size("cols"))
    row_ref[...] = key_row
    bias_ref[...] = jnp.where(near, 0.0, -1e30)


def main_kernel(
    gain_ref, own_ref, far_ref, kn_ref, vn_ref, qn_ref, don_ref, kraw_ref, qraw_ref, normed_ref,
    row_ref, bias_ref, win_ref, wo_ref, scale_ref,
    out_ref, dx_ref, features_ref, send_ref, keep_ref,
    kf_s, vf_s, qf_s, dof_s, att_s, dq_s, dk_s, dv_s, gp_s,
):
    my_row, my_col = lax.axis_index("rows"), lax.axis_index("cols")
    even = my_row % 2 == 0
    first_core = my_col % 2 == 0
    scale = scale_ref[...]
    gain = lane_gain(gain_ref)
    ones = head_ones()
    sub = lax.broadcasted_iota(jnp.int32, (8, 512), 0)
    edge = jnp.where(first_core, 3, 0)

    def far_du(both, third):
        value = jnp.where(sub == edge, both[6:7], 0.0)
        value = jnp.where(sub == edge + 1, both[7:8], value)
        return jnp.where(sub == edge + 2, third, value)

    def rows_far(first_tile):
        return [tile(far_ref, first_tile + j) for j in range(6)]

    c_tiles, d_tiles = rows_far(10), rows_far(16)
    above = [jnp.where(even, d, c) for c, d in zip(c_tiles, d_tiles)]
    below = [jnp.where(even, c, d) for c, d in zip(c_tiles, d_tiles)]
    middle = [tile(far_ref, j) for j in range(8)]
    thirds = tile(far_ref, 8)
    x_far = jnp.concatenate(above + middle + below, axis=0)
    du_far = [far_du(above[j], above[j + 3][6:7]) for j in range(3)]
    du_far += [far_du(middle[j], thirds[j : j + 1]) for j in range(8)]
    du_far += [far_du(below[j], below[j + 3][6:7]) for j in range(3)]
    normed_far = normalize(x_far, scale)
    normed = normed_far.astype(BF16)
    raw = mm(normed, win_ref[:, 512:1024]).astype(BF16).astype(F32)
    kf_s[...] = unit(raw, ones).astype(BF16)
    vf_s[...] = mm(normed, win_ref[:, 1024:1536]).astype(BF16)
    raw = mm(normed_far[24:136].astype(BF16), win_ref[:, 0:512]).astype(BF16).astype(F32)
    qf_s[...] = (unit(raw, ones) * gain).astype(BF16)
    dof_s[...] = mm_nt(jnp.concatenate(du_far, axis=0).astype(BF16), wo_ref[...]).astype(BF16)

    dk_s[...] = jnp.zeros_like(dk_s)
    dv_s[...] = jnp.zeros_like(dv_s)
    for i in range(7):
        image_row = row_ref[...] + (8 * my_row - 6 + 2 * i)
        inside = (image_row >= 0) & (image_row < 8 * lax.axis_size("rows"))
        bias = jnp.where(inside, bias_ref[...], -1e30)
        bias = jnp.concatenate([bias, bias], axis=1)
        blocks = range(max(i, 3), min(i + 4, 7))
        there = slice(32 * (blocks[0] - 3), 32 * (blocks[-1] - 2))

        def own_keys(value):
            parts = [value[NEAR * (b - i) : NEAR * (b - i) + 32] for b in blocks]
            return jnp.concatenate(parts, axis=0)

        for g in range(2):
            lanes = slice(256 * g, 256 * g + 256)

            def keys(near_ref, far_ref):
                parts = [near_ref[NEAR * i : NEAR * (i + 4), lanes], far_ref[FAR * i : FAR * (i + 4), lanes]]
                return jnp.concatenate(parts, axis=0)

            def queries(near_ref, far_ref):
                parts = [near_ref[NEAR * i : NEAR * (i + 1), lanes], far_ref[FAR * i : FAR * (i + 1), lanes]]
                return by_head(jnp.concatenate(parts, axis=0))

            k_t, v_t = keys(kn_ref, kf_s), keys(vn_ref, vf_s)
            q_h, do_h = queries(qn_ref, qf_s), queries(don_ref, dof_s)
            scores = mm_nt(k_t, q_h) + bias
            weight = jnp.exp(scores - jnp.max(scores, axis=0, keepdims=True))
            weight = weight * (1.0 / jnp.sum(weight, axis=0, keepdims=True))
            prob = weight.astype(BF16)
            dprob = mm_nt(v_t, do_h)
            mean = jnp.sum(weight * dprob, axis=0, keepdims=True)
            dscore = (weight * (dprob - mean)).astype(BF16)
            dv_s[there, lanes] += mm(own_keys(prob), do_h)
            dk_s[there, lanes] += mm(own_keys(dscore), q_h)
            if 1 <= i <= 5:
                att = own_heads(mm_tn(prob, v_t)).astype(BF16)
                dq = own_heads(mm_tn(dscore, k_t)).astype(BF16)
                for n in range(2):
                    at = 2 * i + n - 3
                    if 0 <= at < 8:
                        att_s[16 * at : 16 * at + 16, lanes] = att[16 * n : 16 * n + 16]
                        dq_s[16 * at : 16 * at + 16, lanes] = dq[16 * n : 16 * n + 16]

    att = att_s[...]
    normed = normed_ref[...]
    x = own_ref[0:128, :].astype(F32)
    out_ref[...] = (x + mm(att, wo_ref[...])).astype(BF16)

    def norm_back(raw, grad):
        inv = lax.rsqrt(head_sums(raw * raw, ones) + 1e-06)
        return inv * (grad - raw * (inv * inv) * head_sums(raw * grad, ones))

    dq = norm_back(qraw_ref[...].astype(F32), dq_s[...].astype(F32) * gain)
    dk = norm_back(kraw_ref[...].astype(F32), dk_s[...])
    gp_s[:, 0:512] = dq.astype(BF16)
    gp_s[:, 512:1024] = dk.astype(BF16)
    gp_s[:, 1024:1536] = dv_s[...].astype(BF16)
    dnormed = mm_nt(gp_s[...], win_ref[...]) * scale
    r = lax.rsqrt(jnp.mean(x * x, axis=-1, keepdims=True) + 1e-06)
    along = jnp.mean(dnormed * x, axis=-1, keepdims=True)
    dx = r * dnormed - x * (r * r * r * along)
    dx_ref[...] = (own_ref[128:256, :].astype(F32) + dx).astype(BF16)

    features_ref[0:512, :] = jnp.transpose(normed)
    features_ref[512:1024, :] = jnp.transpose(att)
    for core in range(2):

        @pl.when(my_col % 2 == core)
        def _():
            for ref, half in ((keep_ref, core), (send_ref, 1 - core)):
                ref[:, 0:768] = gp_s[:, 768 * half : 768 * half + 768]
                ref[:, 768:1024] = own_ref[128:256, 256 * half : 256 * half + 256]


def grads_kernel(factor, features_ref, keep_ref, got_features_ref, got_ref, out_ref):
    features = jnp.concatenate([features_ref[...], got_features_ref[...]], axis=1)
    grads = jnp.concatenate([keep_ref[...], got_ref[...]], axis=0)
    out_ref[:, 0:768] = (mm(features[:512], grads[:, :768]) * factor).astype(BF16)
    out_ref[:, 768:1024] = (mm(features[512:], grads[:, 768:]) * factor).astype(BF16)


def sum_kernel(rows, parts_ref, out_ref):
    count = parts_ref.shape[0] // rows
    step = max(rows, 16)
    total = parts_ref[0:step, :].astype(F32)
    for i in range(1, count * rows // step):
        total = total + parts_ref[step * i : step * (i + 1), :].astype(F32)
    while total.shape[0] > rows:
        half = total.shape[0] // 2
        total = total[:half] + total[half:]
    block = jnp.concatenate([total] * (step // rows), axis=0).astype(BF16)
    for i in range(count * rows // step):
        out_ref[step * i : step * (i + 1), :] = block


def final_kernel(mine, grads_ref, *refs):
    qkv_ref, out_ref, qkv_s, out_s, sems = refs[-5:]
    steps = sems.shape[1]
    rows = grads_ref.shape[0] // steps
    for core in range(2):

        @pl.when(lax.axis_index("cols") % 2 == core)
        def _():
            half = core if mine else 1 - core
            copies = []
            for i in range(steps):
                part = slice(rows * i, rows * (i + 1))
                qkv_s[part, :] = grads_ref[part, 0:768].astype(F32)
                out_s[part, :] = grads_ref[part, 768:1024].astype(F32)
                lanes = slice(768 * half, 768 * half + 768)
                copies.append(pltpu.make_async_copy(qkv_s.at[part], qkv_ref.at[part, lanes], sems.at[0, i]))
                lanes = slice(256 * half, 256 * half + 256)
                copies.append(pltpu.make_async_copy(out_s.at[part], out_ref.at[part, lanes], sems.at[1, i]))
                copies[-2].start()
                copies[-1].start()
            for copy in copies:
                copy.wait()


def write_half(mine, half_grads, *whole):
    unplaced = pl.BlockSpec(memory_space=pl.ANY)
    return pl.pallas_call(
        functools.partial(final_kernel, mine),
        in_specs=[pl.BlockSpec(memory_space=pltpu.VMEM)] + [unplaced] * len(whole),
        out_specs=[unplaced, unplaced],
        out_shape=[
            jax.ShapeDtypeStruct((512, 1536), F32),
            jax.ShapeDtypeStruct((512, 512), F32),
        ],
        scratch_shapes=[
            pltpu.VMEM((512, 768), F32), pltpu.VMEM((512, 256), F32), pltpu.SemaphoreType.DMA((2, 8)),
        ],
        input_output_aliases={1: 0, 2: 1} if whole else {},
        compiler_params=pltpu.CompilerParams(vmem_limit_bytes=SMALL_LIMIT),
        cost_estimate=pl.CostEstimate(flops=1 << 20, bytes_accessed=3 << 20, transcendentals=0),
    )(half_grads, *whole)


def call(kernel, outs, scratch=(), flops=0, scalars=0, inputs=0, limit=VMEM_LIMIT):
    whole = pl.BlockSpec(memory_space=pltpu.VMEM)
    return pl.pallas_call(
        kernel,
        out_shape=outs,
        in_specs=[pl.BlockSpec(memory_space=pltpu.SMEM)] * scalars
        + [whole] * inputs,
        out_specs=jax.tree.map(lambda _: whole, outs),
        scratch_shapes=list(scratch),
        compiler_params=pltpu.CompilerParams(vmem_limit_bytes=limit),
        cost_estimate=pl.CostEstimate(flops=flops, bytes_accessed=4 << 20, transcendentals=0),
    )


def condition(noise_level_step, label, category_gain_offset, noise_level_gain_matrix):
    half_freqs = noise_level_gain_matrix.shape[0] // 2
    steps_idx = jnp.arange(half_freqs, dtype=F32)
    freq_rates = 2.0 * math.pi * jnp.exp(steps_idx * (math.log(64.0) / half_freqs))
    angles = noise_level_step[0].astype(F32) * 0.001 * freq_rates
    features = jnp.concatenate([jnp.cos(angles), jnp.sin(angles)]).astype(BF16)
    shifted = jnp.dot(features[None, :], noise_level_gain_matrix, preferred_element_type=F32)
    class_row = lax.dynamic_slice_in_dim(category_gain_offset, label[0], 1, 0).astype(F32)
    return 1.0 + class_row + shifted


def swapped(value, row_to, col_to):
    n_rows, n_cols = lax.axis_size("rows"), lax.axis_size("cols")
    pairs = []
    for r in range(n_rows):
        for c in range(n_cols):
            to_row, to_col = row_to(r), col_to(c)
            if 0 <= to_row < n_rows and 0 <= to_col < n_cols:
                pairs.append((r * n_cols + c, to_row * n_cols + to_col))
    return lax.ppermute(value, AXES, pairs)


def same(i):
    return i


def paired(i):
    return i ^ 1


def across(i):
    return i - 1 if i % 2 == 0 else i + 1


def per_device(
    grid_token_states, upstream_gradient, noise_level_step, picture_category_label,
    category_gain_offset, noise_level_gain_matrix, attention_input_matrix,
    final_projection_matrix, cosine_logit_gain,
):
    x, du = grid_token_states, upstream_gradient
    height, columns, width = x.shape
    n_rows, n_cols = lax.axis_size("rows"), lax.axis_size("cols")
    tokens = height * columns
    bf = lambda *shape: jax.ShapeDtypeStruct(shape, BF16)
    vm = pltpu.VMEM
    own = jnp.concatenate([x, du], axis=0).reshape(2 * tokens, width)
    to_c, to_d = call(
        rows_kernel, (bf(144, width), bf(144, width)), inputs=1, limit=SMALL_LIMIT
    )(own)
    from_c = swapped(to_c, paired, same)
    from_d = swapped(to_d, across, same)
    mate = swapped(own, same, paired)
    scale = condition(
        noise_level_step, picture_category_label, category_gain_offset, noise_level_gain_matrix
    )
    mask = call(
        mask_kernel,
        (jax.ShapeDtypeStruct((256, 128), jnp.int32), jax.ShapeDtypeStruct((256, 128), F32)),
        limit=SMALL_LIMIT,
    )()
    to_far, rows = call(
        columns_kernel, (bf(176, width), bf(288, width)), flops=16 << 30, inputs=7, limit=SMALL_LIMIT
    )(own, from_c, from_d, mate, scale, *mask)
    far = swapped(to_far, same, across)
    mate_rows = swapped(rows, same, paired)
    weights = (attention_input_matrix, final_projection_matrix, scale)
    k, v, q, do, kraw, qraw, normed = call(
        near_kernel,
        (bf(480, width), bf(480, width), bf(336, width), bf(336, width), bf(128, width), bf(128, width), bf(128, width)),
        scratch=[vm((320, 512), F32), vm((160, 512), F32), vm((336, 512), BF16)],
        flops=1 << 20, scalars=1, inputs=7,
    )(cosine_logit_gain, own, mate, rows, mate_rows, *weights)

    output, grad_latent, features, send, keep = call(
        main_kernel,
        (bf(tokens, width), bf(tokens, width), bf(1024, tokens), bf(tokens, 1024), bf(tokens, 1024)),
        scratch=[
            vm((160, 512), BF16), vm((160, 512), BF16), vm((112, 512), BF16), vm((112, 512), BF16),
            vm((128, 512), BF16), vm((128, 512), BF16), vm((128, 512), F32), vm((128, 512), F32),
            vm((128, 1536), BF16),
        ],
        flops=8 << 30, scalars=1, inputs=14,
    )(cosine_logit_gain, own, far, k, v, q, do, kraw, qraw, normed, *mask, *weights)

    got_features = swapped(features, same, paired)
    got = swapped(send, same, paired)
    factor = 1.0 / math.sqrt(tokens * n_rows * n_cols)
    partial = call(
        functools.partial(grads_kernel, factor), bf(512, 1024), flops=1 << 29, inputs=4, limit=SMALL_LIMIT
    )(features, keep, got_features, got)

    groups = [
        [r * n_cols + 2 * c + core_ for r in range(n_rows) for c in range(n_cols // 2)]
        for core_ in range(2)
    ]
    members = n_rows * n_cols // 2
    each = 512 // members

    def exchange(value):
        return lax.all_to_all(
            value.reshape(members, each, 1024), AXES, 0, 0, axis_index_groups=groups, tiled=True
        ).reshape(512, 1024)

    summed = call(
        functools.partial(sum_kernel, each), bf(512, 1024), inputs=1, limit=SMALL_LIMIT
    )(exchange(partial))
    mine = exchange(summed)
    other = swapped(mine, same, paired)
    qkv_grad, out_grad = write_half(False, other, *write_half(True, mine))
    return output.reshape(x.shape), grad_latent.reshape(x.shape), qkv_grad, out_grad


def solution(mesh):
    placed = (P("rows", "cols", None), P("rows", "cols", None)) + (P(),) * 7
    return jax.shard_map(
        per_device,
        mesh=mesh,
        in_specs=placed,
        out_specs=(P("rows", "cols", None), P("rows", "cols", None), P(), P()),
        check_vma=False,
    )
```

```python
import functools
import math

import jax
import jax.numpy as jnp
from jax import lax
from jax.experimental import pallas as pl
from jax.experimental.pallas import tpu as pltpu
from jax.sharding import PartitionSpec as P

HEADS = 8
HEAD = 64
BF16 = jnp.bfloat16
F32 = jnp.float32
VMEM_LIMIT = 28 * 1024 * 1024
SMALL_LIMIT = 8 * 1024 * 1024
AXES = ("rows", "cols")
NEAR, FAR = 48, 16


def mm(a, b):
    return jnp.dot(a, b, preferred_element_type=F32)


def mm_nt(a, b):
    return lax.dot_general(a, b, (((1,), (1,)), ((), ())), preferred_element_type=F32)


def mm_tn(a, b):
    return lax.dot_general(a, b, (((0,), (0,)), ((), ())), preferred_element_type=F32)


def head_sums(product, ones):
    high = product.astype(BF16)
    low = (product - high.astype(F32)).astype(BF16)
    parts = []
    for g in range(2):
        lanes = slice(256 * g, 256 * g + 256)
        parts.append(mm(high[:, lanes], ones) + mm(low[:, lanes], ones))
    return jnp.concatenate(parts, axis=1)


def by_head(block):
    head_of = lax.broadcasted_iota(jnp.int32, block.shape, 1) // HEAD
    zero = jnp.zeros_like(block)
    return jnp.concatenate([jnp.where(head_of == h, block, zero) for h in range(4)], axis=0)


def own_heads(result):
    head_of = lax.broadcasted_iota(jnp.int32, (32, 256), 1) // HEAD
    total = result[:32]
    for h in range(1, 4):
        total = jnp.where(head_of == h, result[HEAD * h : HEAD * h + 32], total)
    return total


def head_ones():
    row_head = lax.broadcasted_iota(jnp.int32, (256, 256), 0) // HEAD
    lane_head = lax.broadcasted_iota(jnp.int32, (256, 256), 1) // HEAD
    return jnp.where(row_head == lane_head, 1.0, 0.0).astype(BF16)


def lane_gain(gain_ref):
    head_of = lax.broadcasted_iota(jnp.int32, (1, 512), 1) // HEAD
    gain = jnp.zeros((1, 512), F32)
    for h in range(HEADS):
        gain = jnp.where(head_of == h, gain_ref[h], gain)
    return gain


def block(ref, index):
    return ref[16 * index : 16 * index + 16, :].astype(F32)


def tile(ref, index):
    return block(ref, index // 2)[8 * (index % 2) : 8 * (index % 2) + 8]


def normalize(x, scale):
    return x * lax.rsqrt(jnp.mean(x * x, axis=-1, keepdims=True) + 1e-06) * scale


def unit(raw, ones):
    return raw * lax.rsqrt(head_sums(raw * raw, ones) + 1e-06)


def rows_kernel(own_ref, d_ref, c_ref, copy_ref):
    even = lax.axis_index("rows") % 2 == 0
    copy_ref[...] = own_ref[...]
    for ref, take_last in ((c_ref, even), (d_ref, jnp.logical_not(even))):

        @pl.when(take_last)
        def _():
            ref[0:96, :] = own_ref[32:128, :]
            ref[96:144, :] = own_ref[208:256, :]

        @pl.when(jnp.logical_not(take_last))
        def _():
            ref[0:96, :] = own_ref[0:96, :]
            ref[96:144, :] = own_ref[128:176, :]


def columns_kernel(own_ref, d_ref, c_ref, _mate, _scale, _row, _bias, far_ref, both_ref):
    even = lax.axis_index("rows") % 2 == 0
    first_core = lax.axis_index("cols") % 2 == 0
    sub = lax.broadcasted_iota(jnp.int32, (8, 512), 0)
    both_ref[0:144, :] = c_ref[...]
    both_ref[144:288, :] = d_ref[...]

    def x_edge(x):
        return jnp.where(first_core, x, pltpu.roll(x, 6, 0))[:8]

    def du_edge(du):
        third = jnp.where(first_core, du[2:3], du[15:16])
        return jnp.where(first_core, pltpu.roll(du, 6, 0), pltpu.roll(du, 9, 0))[:8], third

    tiles = []
    thirds = jnp.zeros((8, 512), F32)
    for row in range(8):
        two, third = du_edge(block(own_ref, 8 + row))
        tiles.append(jnp.where(sub < 6, x_edge(block(own_ref, row)), two))
        thirds = jnp.where(sub == row, third, thirds)
    tiles += [thirds, jnp.zeros((8, 512), F32)]
    for ref in (c_ref, d_ref):
        edges = [du_edge(block(ref, 6 + j)) for j in range(3)]
        for j in range(6):
            rest = edges[j][0] if j < 3 else edges[j - 3][1]
            tiles.append(jnp.where(sub < 6, x_edge(block(ref, j)), rest))
    for i in range(11):
        far_ref[16 * i : 16 * i + 16, :] = jnp.concatenate(tiles[2 * i : 2 * i + 2], 0).astype(BF16)


def near_kernel(
    gain_ref, own_ref, mate_ref, rows_ref, mate_rows_ref, win_ref, wo_ref, scale_ref,
    k_ref, v_ref, q_ref, do_ref, kraw_ref, qraw_ref, normed_ref,
    own_s, mate_s, du_s,
):
    even = lax.axis_index("rows") % 2 == 0
    first_core = lax.axis_index("cols") % 2 == 0
    scale = scale_ref[...]
    gain = lane_gain(gain_ref)
    ones = head_ones()

    def pick(low, high, above):
        return jnp.where(even, high, low) if above else jnp.where(even, low, high)

    def row_parts(row, first):
        if 0 <= row < 8:
            own, mate = block(own_ref, first + row), block(mate_ref, first + row)
        else:
            above = row < 0
            j = (row + (6 if above else -8)) if first == 0 else 6 + (row + (3 if above else -8))
            own = pick(block(rows_ref, j), block(rows_ref, 9 + j), above)
            mate = pick(block(mate_rows_ref, j), block(mate_rows_ref, 9 + j), above)
        return own, jnp.where(first_core, mate[:8], mate[8:])

    for e in range(20):
        own, mate = row_parts(e - 6, 0)
        own_s[16 * e : 16 * e + 16, :] = normalize(own, scale)
        mate_s[8 * e : 8 * e + 8, :] = normalize(mate, scale)
    normed_ref[...] = own_s[96:224, :].astype(BF16)
    for i in range(7):
        first, second = row_parts(2 * i - 3, 8), row_parts(2 * i - 2, 8)
        pair = jnp.concatenate([first[0], second[0], first[1], second[1]], axis=0)
        du_s[NEAR * i : NEAR * (i + 1), :] = pair.astype(BF16)

    def normed_pairs(first_row, count):
        parts = []
        for n in range(count):
            row = first_row + 2 * n
            parts += [own_s[16 * row : 16 * row + 32, :], mate_s[8 * row : 8 * row + 16, :]]
        return jnp.concatenate(parts, axis=0).astype(BF16)

    for t in range(5):
        rows = slice(96 * t, 96 * t + 96)
        normed = normed_pairs(4 * t, 2)
        raw = mm(normed, win_ref[:, 512:1024]).astype(BF16).astype(F32)
        k_ref[rows, :] = unit(raw, ones).astype(BF16)
        v_ref[rows, :] = mm(normed, win_ref[:, 1024:1536]).astype(BF16)
        for n in range(2):
            at = 2 * t + n - 3
            if 0 <= at < 4:
                kraw_ref[32 * at : 32 * at + 32, :] = raw[48 * n : 48 * n + 32].astype(BF16)
    for first, count in ((0, 2), (2, 2), (4, 2), (6, 1)):
        rows = slice(NEAR * first, NEAR * (first + count))
        normed = normed_pairs(3 + 2 * first, count)
        raw = mm(normed, win_ref[:, 0:512]).astype(BF16).astype(F32)
        q_ref[rows, :] = (unit(raw, ones) * gain).astype(BF16)
        do_ref[rows, :] = mm_nt(du_s[rows, :], wo_ref[...]).astype(BF16)
        for n in range(2 * count):
            at = 2 * first + n - 3
            if 0 <= at < 8:
                here = 48 * (n // 2) + 16 * (n % 2)
                qraw_ref[16 * at : 16 * at + 16, :] = raw[here : here + 16].astype(BF16)


def mask_kernel(row_ref, bias_ref):
    my_col = lax.axis_index("cols")
    first_core = my_col % 2 == 0
    mate_base = jnp.where(first_core, 16, -8)
    far_base = jnp.where(first_core, -6, 16)

    def places(index, near):
        in_near = index < near
        pair = jnp.where(in_near, index // NEAR, 0)
        j = jnp.where(in_near, index % NEAR, index - near)
        mine = in_near & (j < 32)
        eights = jnp.where(in_near, j - 32, j)
        row = jnp.where(mine, 2 * pair + j // 16, 2 * pair + eights // 8)
        slot = eights % 8
        far_col = jnp.where(slot < 6, far_base + slot, 1000)
        return row, jnp.where(mine, j % 16, jnp.where(in_near, mate_base + slot, far_col))

    key_row, key_col = places(lax.broadcasted_iota(jnp.int32, (256, 128), 0), 4 * NEAR)
    query_row, query_col = places(lax.broadcasted_iota(jnp.int32, (256, 128), 1) % 64, NEAR)
    row_gap, col_gap = key_row - query_row, key_col - query_col
    near = (row_gap >= 0) & (row_gap <= 6) & (col_gap >= -3) & (col_gap <= 3) & (key_col < 1000)
    image_col = key_col + 16 * my_col
    near = near & (image_col >= 0) & (image_col < 16 * lax.axis_size("cols"))
    row_ref[...] = key_row
    bias_ref[...] = jnp.where(near, 0.0, -1e30)


def main_kernel(
    gain_ref, own_ref, far_ref, kn_ref, vn_ref, qn_ref, don_ref, kraw_ref, qraw_ref, normed_ref,
    row_ref, bias_ref, win_ref, wo_ref, scale_ref,
    out_ref, dx_ref, features_ref, send_ref, keep_ref,
    kf_s, vf_s, qf_s, dof_s, att_s, dq_s, dk_s, dv_s, gp_s,
):
    my_row, my_col = lax.axis_index("rows"), lax.axis_index("cols")
    even = my_row % 2 == 0
    first_core = my_col % 2 == 0
    scale = scale_ref[...]
    gain = lane_gain(gain_ref)
    ones = head_ones()
    sub = lax.broadcasted_iota(jnp.int32, (8, 512), 0)
    edge = jnp.where(first_core, 3, 0)

    def far_du(both, third):
        value = jnp.where(sub == edge, both[6:7], 0.0)
        value = jnp.where(sub == edge + 1, both[7:8], value)
        return jnp.where(sub == edge + 2, third, value)

    def rows_far(first_tile):
        return [tile(far_ref, first_tile + j) for j in range(6)]

    c_tiles, d_tiles = rows_far(10), rows_far(16)
    above = [jnp.where(even, d, c) for c, d in zip(c_tiles, d_tiles)]
    below = [jnp.where(even, c, d) for c, d in zip(c_tiles, d_tiles)]
    middle = [tile(far_ref, j) for j in range(8)]
    thirds = tile(far_ref, 8)
    x_far = jnp.concatenate(above + middle + below, axis=0)
    du_far = [far_du(above[j], above[j + 3][6:7]) for j in range(3)]
    du_far += [far_du(middle[j], thirds[j : j + 1]) for j in range(8)]
    du_far += [far_du(below[j], below[j + 3][6:7]) for j in range(3)]
    normed_far = normalize(x_far, scale)
    normed = normed_far.astype(BF16)
    raw = mm(normed, win_ref[:, 512:1024]).astype(BF16).astype(F32)
    kf_s[...] = unit(raw, ones).astype(BF16)
    vf_s[...] = mm(normed, win_ref[:, 1024:1536]).astype(BF16)
    raw = mm(normed_far[24:136].astype(BF16), win_ref[:, 0:512]).astype(BF16).astype(F32)
    qf_s[...] = (unit(raw, ones) * gain).astype(BF16)
    dof_s[...] = mm_nt(jnp.concatenate(du_far, axis=0).astype(BF16), wo_ref[...]).astype(BF16)

    dk_s[...] = jnp.zeros_like(dk_s)
    dv_s[...] = jnp.zeros_like(dv_s)
    for i in range(7):
        image_row = row_ref[...] + (8 * my_row - 6 + 2 * i)
        inside = (image_row >= 0) & (image_row < 8 * lax.axis_size("rows"))
        bias = jnp.where(inside, bias_ref[...], -1e30)
        bias = jnp.concatenate([bias, bias], axis=1)
        blocks = range(max(i, 3), min(i + 4, 7))
        there = slice(32 * (blocks[0] - 3), 32 * (blocks[-1] - 2))

        def own_keys(value):
            parts = [value[NEAR * (b - i) : NEAR * (b - i) + 32] for b in blocks]
            return jnp.concatenate(parts, axis=0)

        for g in range(2):
            lanes = slice(256 * g, 256 * g + 256)

            def keys(near_ref, far_ref):
                parts = [near_ref[NEAR * i : NEAR * (i + 4), lanes], far_ref[FAR * i : FAR * (i + 4), lanes]]
                return jnp.concatenate(parts, axis=0)

            def queries(near_ref, far_ref):
                parts = [near_ref[NEAR * i : NEAR * (i + 1), lanes], far_ref[FAR * i : FAR * (i + 1), lanes]]
                return by_head(jnp.concatenate(parts, axis=0))

            k_t, v_t = keys(kn_ref, kf_s), keys(vn_ref, vf_s)
            q_h, do_h = queries(qn_ref, qf_s), queries(don_ref, dof_s)
            scores = mm_nt(k_t, q_h) + bias
            weight = jnp.exp(scores - jnp.max(scores, axis=0, keepdims=True))
            weight = weight * (1.0 / jnp.sum(weight, axis=0, keepdims=True))
            prob = weight.astype(BF16)
            dprob = mm_nt(v_t, do_h)
            mean = jnp.sum(weight * dprob, axis=0, keepdims=True)
            dscore = (weight * (dprob - mean)).astype(BF16)
            dv_s[there, lanes] += mm(own_keys(prob), do_h)
            dk_s[there, lanes] += mm(own_keys(dscore), q_h)
            if 1 <= i <= 5:
                att = own_heads(mm_tn(prob, v_t)).astype(BF16)
                dq = own_heads(mm_tn(dscore, k_t)).astype(BF16)
                for n in range(2):
                    at = 2 * i + n - 3
                    if 0 <= at < 8:
                        att_s[16 * at : 16 * at + 16, lanes] = att[16 * n : 16 * n + 16]
                        dq_s[16 * at : 16 * at + 16, lanes] = dq[16 * n : 16 * n + 16]

    att = att_s[...]
    normed = normed_ref[...]
    x = own_ref[0:128, :].astype(F32)
    out_ref[...] = (x + mm(att, wo_ref[...])).astype(BF16)

    def norm_back(raw, grad):
        inv = lax.rsqrt(head_sums(raw * raw, ones) + 1e-06)
        return inv * (grad - raw * (inv * inv) * head_sums(raw * grad, ones))

    dq = norm_back(qraw_ref[...].astype(F32), dq_s[...].astype(F32) * gain)
    dk = norm_back(kraw_ref[...].astype(F32), dk_s[...])
    gp_s[:, 0:512] = dq.astype(BF16)
    gp_s[:, 512:1024] = dk.astype(BF16)
    gp_s[:, 1024:1536] = dv_s[...].astype(BF16)
    dnormed = mm_nt(gp_s[...], win_ref[...]) * scale
    r = lax.rsqrt(jnp.mean(x * x, axis=-1, keepdims=True) + 1e-06)
    along = jnp.mean(dnormed * x, axis=-1, keepdims=True)
    dx = r * dnormed - x * (r * r * r * along)
    dx_ref[...] = (own_ref[128:256, :].astype(F32) + dx).astype(BF16)

    features_ref[0:512, :] = jnp.transpose(normed)
    features_ref[512:1024, :] = jnp.transpose(att)
    for core in range(2):

        @pl.when(my_col % 2 == core)
        def _():
            for ref, half in ((keep_ref, core), (send_ref, 1 - core)):
                ref[:, 0:768] = gp_s[:, 768 * half : 768 * half + 768]
                ref[:, 768:1024] = own_ref[128:256, 256 * half : 256 * half + 256]


def grads_kernel(factor, features_ref, keep_ref, got_features_ref, got_ref, out_ref):
    features = jnp.concatenate([features_ref[...], got_features_ref[...]], axis=1)
    grads = jnp.concatenate([keep_ref[...], got_ref[...]], axis=0)
    out_ref[:, 0:768] = (mm(features[:512], grads[:, :768]) * factor).astype(BF16)
    out_ref[:, 768:1024] = (mm(features[512:], grads[:, 768:]) * factor).astype(BF16)


def sum_kernel(rows, parts_ref, out_ref):
    count = parts_ref.shape[0] // rows
    step = max(rows, 16)
    total = parts_ref[0:step, :].astype(F32)
    for i in range(1, count * rows // step):
        total = total + parts_ref[step * i : step * (i + 1), :].astype(F32)
    while total.shape[0] > rows:
        half = total.shape[0] // 2
        total = total[:half] + total[half:]
    block = jnp.concatenate([total] * (step // rows), axis=0).astype(BF16)
    for i in range(count * rows // step):
        out_ref[step * i : step * (i + 1), :] = block


def final_kernel(mine, grads_ref, *refs):
    qkv_ref, out_ref, qkv_s, out_s, sems = refs[-5:]
    steps = sems.shape[1]
    rows = grads_ref.shape[0] // steps
    for core in range(2):

        @pl.when(lax.axis_index("cols") % 2 == core)
        def _():
            half = core if mine else 1 - core
            copies = []
            for i in range(steps):
                part = slice(rows * i, rows * (i + 1))
                qkv_s[part, :] = grads_ref[part, 0:768].astype(F32)
                out_s[part, :] = grads_ref[part, 768:1024].astype(F32)
                lanes = slice(768 * half, 768 * half + 768)
                copies.append(pltpu.make_async_copy(qkv_s.at[part], qkv_ref.at[part, lanes], sems.at[0, i]))
                lanes = slice(256 * half, 256 * half + 256)
                copies.append(pltpu.make_async_copy(out_s.at[part], out_ref.at[part, lanes], sems.at[1, i]))
                copies[-2].start()
                copies[-1].start()
            for copy in copies:
                copy.wait()


def write_half(mine, half_grads, *whole):
    unplaced = pl.BlockSpec(memory_space=pl.ANY)
    return pl.pallas_call(
        functools.partial(final_kernel, mine),
        in_specs=[pl.BlockSpec(memory_space=pltpu.VMEM)] + [unplaced] * len(whole),
        out_specs=[unplaced, unplaced],
        out_shape=[
            jax.ShapeDtypeStruct((512, 1536), F32),
            jax.ShapeDtypeStruct((512, 512), F32),
        ],
        scratch_shapes=[
            pltpu.VMEM((512, 768), F32), pltpu.VMEM((512, 256), F32), pltpu.SemaphoreType.DMA((2, 8)),
        ],
        input_output_aliases={1: 0, 2: 1} if whole else {},
        compiler_params=pltpu.CompilerParams(vmem_limit_bytes=SMALL_LIMIT),
        cost_estimate=pl.CostEstimate(flops=1 << 20, bytes_accessed=3 << 20, transcendentals=0),
    )(half_grads, *whole)


def call(kernel, outs, scratch=(), flops=0, scalars=0, inputs=0, limit=VMEM_LIMIT):
    whole = pl.BlockSpec(memory_space=pltpu.VMEM)
    return pl.pallas_call(
        kernel,
        out_shape=outs,
        in_specs=[pl.BlockSpec(memory_space=pltpu.SMEM)] * scalars
        + [whole] * inputs,
        out_specs=jax.tree.map(lambda _: whole, outs),
        scratch_shapes=list(scratch),
        compiler_params=pltpu.CompilerParams(vmem_limit_bytes=limit),
        cost_estimate=pl.CostEstimate(flops=flops, bytes_accessed=4 << 20, transcendentals=0),
    )


def condition(noise_level_step, label, category_gain_offset, noise_level_gain_matrix):
    half_freqs = noise_level_gain_matrix.shape[0] // 2
    steps_idx = jnp.arange(half_freqs, dtype=F32)
    freq_rates = 2.0 * math.pi * jnp.exp(steps_idx * (math.log(64.0) / half_freqs))
    angles = noise_level_step[0].astype(F32) * 0.001 * freq_rates
    features = jnp.concatenate([jnp.cos(angles), jnp.sin(angles)]).astype(BF16)
    shifted = jnp.dot(features[None, :], noise_level_gain_matrix, preferred_element_type=F32)
    class_row = lax.dynamic_slice_in_dim(category_gain_offset, label[0], 1, 0).astype(F32)
    return 1.0 + class_row + shifted


def swapped(value, row_to, col_to):
    n_rows, n_cols = lax.axis_size("rows"), lax.axis_size("cols")
    pairs = []
    for r in range(n_rows):
        for c in range(n_cols):
            to_row, to_col = row_to(r), col_to(c)
            if 0 <= to_row < n_rows and 0 <= to_col < n_cols:
                pairs.append((r * n_cols + c, to_row * n_cols + to_col))
    return lax.ppermute(value, AXES, pairs)


def same(i):
    return i


def paired(i):
    return i ^ 1


def across(i):
    return i - 1 if i % 2 == 0 else i + 1


def per_device(
    grid_token_states, upstream_gradient, noise_level_step, picture_category_label,
    category_gain_offset, noise_level_gain_matrix, attention_input_matrix,
    final_projection_matrix, cosine_logit_gain,
):
    x, du = grid_token_states, upstream_gradient
    height, columns, width = x.shape
    n_rows, n_cols = lax.axis_size("rows"), lax.axis_size("cols")
    tokens = height * columns
    bf = lambda *shape: jax.ShapeDtypeStruct(shape, BF16)
    vm = pltpu.VMEM
    own = jnp.concatenate([x, du], axis=0).reshape(2 * tokens, width)
    to_d, to_c, own = call(
        rows_kernel, (bf(144, width), bf(144, width), bf(256, width)), inputs=1, limit=SMALL_LIMIT
    )(own)
    from_d = swapped(to_d, across, same)
    from_c = swapped(to_c, paired, same)
    mate = swapped(own, same, paired)
    scale = condition(
        noise_level_step, picture_category_label, category_gain_offset, noise_level_gain_matrix
    )
    mask = call(
        mask_kernel,
        (jax.ShapeDtypeStruct((256, 128), jnp.int32), jax.ShapeDtypeStruct((256, 128), F32)),
        limit=SMALL_LIMIT,
    )()
    to_far, rows = call(
        columns_kernel, (bf(176, width), bf(288, width)), flops=16 << 30, inputs=7, limit=SMALL_LIMIT
    )(own, from_d, from_c, mate, scale, *mask)
    far = swapped(to_far, same, across)
    mate_rows = swapped(rows, same, paired)
    weights = (attention_input_matrix, final_projection_matrix, scale)
    k, v, q, do, kraw, qraw, normed = call(
        near_kernel,
        (bf(480, width), bf(480, width), bf(336, width), bf(336, width), bf(128, width), bf(128, width), bf(128, width)),
        scratch=[vm((320, 512), F32), vm((160, 512), F32), vm((336, 512), BF16)],
        flops=1 << 20, scalars=1, inputs=7,
    )(cosine_logit_gain, own, mate, rows, mate_rows, *weights)

    output, grad_latent, features, send, keep = call(
        main_kernel,
        (bf(tokens, width), bf(tokens, width), bf(1024, tokens), bf(tokens, 1024), bf(tokens, 1024)),
        scratch=[
            vm((160, 512), BF16), vm((160, 512), BF16), vm((112, 512), BF16), vm((112, 512), BF16),
            vm((128, 512), BF16), vm((128, 512), BF16), vm((128, 512), F32), vm((128, 512), F32),
            vm((128, 1536), BF16),
        ],
        flops=8 << 30, scalars=1, inputs=14,
    )(cosine_logit_gain, own, far, k, v, q, do, kraw, qraw, normed, *mask, *weights)

    got_features = swapped(features, same, paired)
    got = swapped(send, same, paired)
    factor = 1.0 / math.sqrt(tokens * n_rows * n_cols)
    partial = call(
        functools.partial(grads_kernel, factor), bf(512, 1024), flops=1 << 29, inputs=4, limit=SMALL_LIMIT
    )(features, keep, got_features, got)

    groups = [
        [r * n_cols + 2 * c + core_ for r in range(n_rows) for c in range(n_cols // 2)]
        for core_ in range(2)
    ]
    members = n_rows * n_cols // 2
    each = 512 // members

    def exchange(value):
        return lax.all_to_all(
            value.reshape(members, each, 1024), AXES, 0, 0, axis_index_groups=groups, tiled=True
        ).reshape(512, 1024)

    summed = call(
        functools.partial(sum_kernel, each), bf(512, 1024), inputs=1, limit=SMALL_LIMIT
    )(exchange(partial))
    mine = exchange(summed)
    other = swapped(mine, same, paired)
    qkv_grad, out_grad = write_half(False, other, *write_half(True, mine))
    return output.reshape(x.shape), grad_latent.reshape(x.shape), qkv_grad, out_grad


def solution(mesh):
    placed = (P("rows", "cols", None), P("rows", "cols", None)) + (P(),) * 7
    return jax.shard_map(
        per_device,
        mesh=mesh,
        in_specs=placed,
        out_specs=(P("rows", "cols", None), P("rows", "cols", None), P(), P()),
        check_vma=False,
    )
```

```python
import functools
import math

import jax
import jax.numpy as jnp
from jax import lax
from jax.experimental import pallas as pl
from jax.experimental.pallas import tpu as pltpu
from jax.sharding import PartitionSpec as P

HEADS = 8
HEAD = 64
BF16 = jnp.bfloat16
F32 = jnp.float32
VMEM_LIMIT = 28 * 1024 * 1024
SMALL_LIMIT = 8 * 1024 * 1024
AXES = ("rows", "cols")
NEAR, FAR = 48, 16


def mm(a, b):
    return jnp.dot(a, b, preferred_element_type=F32)


def mm_nt(a, b):
    return lax.dot_general(a, b, (((1,), (1,)), ((), ())), preferred_element_type=F32)


def mm_tn(a, b):
    return lax.dot_general(a, b, (((0,), (0,)), ((), ())), preferred_element_type=F32)


def head_sums(product, ones):
    high = product.astype(BF16)
    low = (product - high.astype(F32)).astype(BF16)
    parts = []
    for g in range(2):
        lanes = slice(256 * g, 256 * g + 256)
        parts.append(mm(high[:, lanes], ones) + mm(low[:, lanes], ones))
    return jnp.concatenate(parts, axis=1)


def by_head(block):
    head_of = lax.broadcasted_iota(jnp.int32, block.shape, 1) // HEAD
    zero = jnp.zeros_like(block)
    return jnp.concatenate([jnp.where(head_of == h, block, zero) for h in range(4)], axis=0)


def own_heads(result):
    head_of = lax.broadcasted_iota(jnp.int32, (32, 256), 1) // HEAD
    total = result[:32]
    for h in range(1, 4):
        total = jnp.where(head_of == h, result[HEAD * h : HEAD * h + 32], total)
    return total


def head_ones():
    row_head = lax.broadcasted_iota(jnp.int32, (256, 256), 0) // HEAD
    lane_head = lax.broadcasted_iota(jnp.int32, (256, 256), 1) // HEAD
    return jnp.where(row_head == lane_head, 1.0, 0.0).astype(BF16)


def lane_gain(gain_ref):
    head_of = lax.broadcasted_iota(jnp.int32, (1, 512), 1) // HEAD
    gain = jnp.zeros((1, 512), F32)
    for h in range(HEADS):
        gain = jnp.where(head_of == h, gain_ref[h], gain)
    return gain


def block(ref, index):
    return ref[16 * index : 16 * index + 16, :].astype(F32)


def tile(ref, index):
    return block(ref, index // 2)[8 * (index % 2) : 8 * (index % 2) + 8]


def normalize(x, scale):
    return x * lax.rsqrt(jnp.mean(x * x, axis=-1, keepdims=True) + 1e-06) * scale


def unit(raw, ones):
    return raw * lax.rsqrt(head_sums(raw * raw, ones) + 1e-06)


def rows_kernel(own_ref, c_ref, d_ref, copy_ref):
    even = lax.axis_index("rows") % 2 == 0
    copy_ref[...] = own_ref[...]
    for ref, take_last in ((c_ref, even), (d_ref, jnp.logical_not(even))):

        @pl.when(take_last)
        def _():
            ref[0:96, :] = own_ref[32:128, :]
            ref[96:144, :] = own_ref[208:256, :]

        @pl.when(jnp.logical_not(take_last))
        def _():
            ref[0:96, :] = own_ref[0:96, :]
            ref[96:144, :] = own_ref[128:176, :]


def columns_kernel(own_ref, c_ref, d_ref, _mate, _scale, _row, _bias, far_ref, both_ref):
    even = lax.axis_index("rows") % 2 == 0
    first_core = lax.axis_index("cols") % 2 == 0
    sub = lax.broadcasted_iota(jnp.int32, (8, 512), 0)
    both_ref[0:144, :] = c_ref[...]
    both_ref[144:288, :] = d_ref[...]

    def x_edge(x):
        return jnp.where(first_core, x, pltpu.roll(x, 6, 0))[:8]

    def du_edge(du):
        third = jnp.where(first_core, du[2:3], du[15:16])
        return jnp.where(first_core, pltpu.roll(du, 6, 0), pltpu.roll(du, 9, 0))[:8], third

    tiles = []
    thirds = jnp.zeros((8, 512), F32)
    for row in range(8):
        two, third = du_edge(block(own_ref, 8 + row))
        tiles.append(jnp.where(sub < 6, x_edge(block(own_ref, row)), two))
        thirds = jnp.where(sub == row, third, thirds)
    tiles += [thirds, jnp.zeros((8, 512), F32)]
    for ref in (c_ref, d_ref):
        edges = [du_edge(block(ref, 6 + j)) for j in range(3)]
        for j in range(6):
            rest = edges[j][0] if j < 3 else edges[j - 3][1]
            tiles.append(jnp.where(sub < 6, x_edge(block(ref, j)), rest))
    for i in range(11):
        far_ref[16 * i : 16 * i + 16, :] = jnp.concatenate(tiles[2 * i : 2 * i + 2], 0).astype(BF16)


def near_kernel(
    gain_ref, own_ref, mate_ref, rows_ref, mate_rows_ref, win_ref, wo_ref, scale_ref,
    k_ref, v_ref, q_ref, do_ref, kraw_ref, qraw_ref, normed_ref,
    own_s, mate_s, du_s,
):
    even = lax.axis_index("rows") % 2 == 0
    first_core = lax.axis_index("cols") % 2 == 0
    scale = scale_ref[...]
    gain = lane_gain(gain_ref)
    ones = head_ones()

    def pick(low, high, above):
        return jnp.where(even, high, low) if above else jnp.where(even, low, high)

    def row_parts(row, first):
        if 0 <= row < 8:
            own, mate = block(own_ref, first + row), block(mate_ref, first + row)
        else:
            above = row < 0
            j = (row + (6 if above else -8)) if first == 0 else 6 + (row + (3 if above else -8))
            own = pick(block(rows_ref, j), block(rows_ref, 9 + j), above)
            mate = pick(block(mate_rows_ref, j), block(mate_rows_ref, 9 + j), above)
        return own, jnp.where(first_core, mate[:8], mate[8:])

    for e in range(20):
        own, mate = row_parts(e - 6, 0)
        own_s[16 * e : 16 * e + 16, :] = normalize(own, scale)
        mate_s[8 * e : 8 * e + 8, :] = normalize(mate, scale)
    normed_ref[...] = own_s[96:224, :].astype(BF16)
    for i in range(7):
        first, second = row_parts(2 * i - 3, 8), row_parts(2 * i - 2, 8)
        pair = jnp.concatenate([first[0], second[0], first[1], second[1]], axis=0)
        du_s[NEAR * i : NEAR * (i + 1), :] = pair.astype(BF16)

    def normed_pairs(first_row, count):
        parts = []
        for n in range(count):
            row = first_row + 2 * n
            parts += [own_s[16 * row : 16 * row + 32, :], mate_s[8 * row : 8 * row + 16, :]]
        return jnp.concatenate(parts, axis=0).astype(BF16)

    for t in range(5):
        rows = slice(96 * t, 96 * t + 96)
        normed = normed_pairs(4 * t, 2)
        raw = mm(normed, win_ref[:, 512:1024]).astype(BF16).astype(F32)
        k_ref[rows, :] = unit(raw, ones).astype(BF16)
        v_ref[rows, :] = mm(normed, win_ref[:, 1024:1536]).astype(BF16)
        for n in range(2):
            at = 2 * t + n - 3
            if 0 <= at < 4:
                kraw_ref[32 * at : 32 * at + 32, :] = raw[48 * n : 48 * n + 32].astype(BF16)
    for first, count in ((0, 2), (2, 2), (4, 2), (6, 1)):
        rows = slice(NEAR * first, NEAR * (first + count))
        normed = normed_pairs(3 + 2 * first, count)
        raw = mm(normed, win_ref[:, 0:512]).astype(BF16).astype(F32)
        q_ref[rows, :] = (unit(raw, ones) * gain).astype(BF16)
        do_ref[rows, :] = mm_nt(du_s[rows, :], wo_ref[...]).astype(BF16)
        for n in range(2 * count):
            at = 2 * first + n - 3
            if 0 <= at < 8:
                here = 48 * (n // 2) + 16 * (n % 2)
                qraw_ref[16 * at : 16 * at + 16, :] = raw[here : here + 16].astype(BF16)


def mask_kernel(row_ref, bias_ref):
    my_col = lax.axis_index("cols")
    first_core = my_col % 2 == 0
    mate_base = jnp.where(first_core, 16, -8)
    far_base = jnp.where(first_core, -6, 16)

    def places(index, near):
        in_near = index < near
        pair = jnp.where(in_near, index // NEAR, 0)
        j = jnp.where(in_near, index % NEAR, index - near)
        mine = in_near & (j < 32)
        eights = jnp.where(in_near, j - 32, j)
        row = jnp.where(mine, 2 * pair + j // 16, 2 * pair + eights // 8)
        slot = eights % 8
        far_col = jnp.where(slot < 6, far_base + slot, 1000)
        return row, jnp.where(mine, j % 16, jnp.where(in_near, mate_base + slot, far_col))

    key_row, key_col = places(lax.broadcasted_iota(jnp.int32, (256, 128), 0), 4 * NEAR)
    query_row, query_col = places(lax.broadcasted_iota(jnp.int32, (256, 128), 1) % 64, NEAR)
    row_gap, col_gap = key_row - query_row, key_col - query_col
    near = (row_gap >= 0) & (row_gap <= 6) & (col_gap >= -3) & (col_gap <= 3) & (key_col < 1000)
    image_col = key_col + 16 * my_col
    near = near & (image_col >= 0) & (image_col < 16 * lax.axis_size("cols"))
    row_ref[...] = key_row
    bias_ref[...] = jnp.where(near, 0.0, -1e30)


def main_kernel(
    gain_ref, own_ref, far_ref, kn_ref, vn_ref, qn_ref, don_ref, kraw_ref, qraw_ref, normed_ref,
    row_ref, bias_ref, win_ref, wo_ref, scale_ref,
    out_ref, dx_ref, send_ref, keep_ref,
    out_s, dx_s, sems, kf_s, vf_s, qf_s, dof_s, att_s, dq_s, dk_s, dv_s, gp_s,
):
    my_row, my_col = lax.axis_index("rows"), lax.axis_index("cols")
    even = my_row % 2 == 0
    first_core = my_col % 2 == 0
    scale = scale_ref[...]
    gain = lane_gain(gain_ref)
    ones = head_ones()
    sub = lax.broadcasted_iota(jnp.int32, (8, 512), 0)
    edge = jnp.where(first_core, 3, 0)

    def far_du(both, third):
        value = jnp.where(sub == edge, both[6:7], 0.0)
        value = jnp.where(sub == edge + 1, both[7:8], value)
        return jnp.where(sub == edge + 2, third, value)

    def rows_far(first_tile):
        return [tile(far_ref, first_tile + j) for j in range(6)]

    c_tiles, d_tiles = rows_far(10), rows_far(16)
    above = [jnp.where(even, d, c) for c, d in zip(c_tiles, d_tiles)]
    below = [jnp.where(even, c, d) for c, d in zip(c_tiles, d_tiles)]
    middle = [tile(far_ref, j) for j in range(8)]
    thirds = tile(far_ref, 8)
    x_far = jnp.concatenate(above + middle + below, axis=0)
    du_far = [far_du(above[j], above[j + 3][6:7]) for j in range(3)]
    du_far += [far_du(middle[j], thirds[j : j + 1]) for j in range(8)]
    du_far += [far_du(below[j], below[j + 3][6:7]) for j in range(3)]
    normed_far = normalize(x_far, scale)
    normed = normed_far.astype(BF16)
    raw = mm(normed, win_ref[:, 512:1024]).astype(BF16).astype(F32)
    kf_s[...] = unit(raw, ones).astype(BF16)
    vf_s[...] = mm(normed, win_ref[:, 1024:1536]).astype(BF16)
    raw = mm(normed_far[24:136].astype(BF16), win_ref[:, 0:512]).astype(BF16).astype(F32)
    qf_s[...] = (unit(raw, ones) * gain).astype(BF16)
    dof_s[...] = mm_nt(jnp.concatenate(du_far, axis=0).astype(BF16), wo_ref[...]).astype(BF16)

    dk_s[...] = jnp.zeros_like(dk_s)
    dv_s[...] = jnp.zeros_like(dv_s)
    for i in range(7):
        image_row = row_ref[...] + (8 * my_row - 6 + 2 * i)
        inside = (image_row >= 0) & (image_row < 8 * lax.axis_size("rows"))
        bias = jnp.where(inside, bias_ref[...], -1e30)
        bias = jnp.concatenate([bias, bias], axis=1)
        blocks = range(max(i, 3), min(i + 4, 7))
        there = slice(32 * (blocks[0] - 3), 32 * (blocks[-1] - 2))

        def own_keys(value):
            parts = [value[NEAR * (b - i) : NEAR * (b - i) + 32] for b in blocks]
            return jnp.concatenate(parts, axis=0)

        for g in range(2):
            lanes = slice(256 * g, 256 * g + 256)

            def keys(near_ref, far_ref):
                parts = [near_ref[NEAR * i : NEAR * (i + 4), lanes], far_ref[FAR * i : FAR * (i + 4), lanes]]
                return jnp.concatenate(parts, axis=0)

            def queries(near_ref, far_ref):
                parts = [near_ref[NEAR * i : NEAR * (i + 1), lanes], far_ref[FAR * i : FAR * (i + 1), lanes]]
                return by_head(jnp.concatenate(parts, axis=0))

            k_t, v_t = keys(kn_ref, kf_s), keys(vn_ref, vf_s)
            q_h, do_h = queries(qn_ref, qf_s), queries(don_ref, dof_s)
            scores = mm_nt(k_t, q_h) + bias
            weight = jnp.exp(scores - jnp.max(scores, axis=0, keepdims=True))
            weight = weight * (1.0 / jnp.sum(weight, axis=0, keepdims=True))
            prob = weight.astype(BF16)
            dprob = mm_nt(v_t, do_h)
            mean = jnp.sum(weight * dprob, axis=0, keepdims=True)
            dscore = (weight * (dprob - mean)).astype(BF16)
            dv_s[there, lanes] += mm(own_keys(prob), do_h)
            dk_s[there, lanes] += mm(own_keys(dscore), q_h)
            if 1 <= i <= 5:
                att = own_heads(mm_tn(prob, v_t)).astype(BF16)
                dq = own_heads(mm_tn(dscore, k_t)).astype(BF16)
                for n in range(2):
                    at = 2 * i + n - 3
                    if 0 <= at < 8:
                        att_s[16 * at : 16 * at + 16, lanes] = att[16 * n : 16 * n + 16]
                        dq_s[16 * at : 16 * at + 16, lanes] = dq[16 * n : 16 * n + 16]

    att = att_s[...]
    normed = normed_ref[...]
    x = own_ref[0:128, :].astype(F32)
    out_s[...] = (x + mm(att, wo_ref[...])).astype(BF16)
    copies = [pltpu.make_async_copy(out_s, out_ref, sems.at[0]), pltpu.make_async_copy(dx_s, dx_ref, sems.at[1])]
    copies[0].start()
    send_ref[0:512, :] = jnp.transpose(normed)
    send_ref[512:1024, :] = jnp.transpose(att)

    def norm_back(raw, grad):
        inv = lax.rsqrt(head_sums(raw * raw, ones) + 1e-06)
        return inv * (grad - raw * (inv * inv) * head_sums(raw * grad, ones))

    dq = norm_back(qraw_ref[...].astype(F32), dq_s[...].astype(F32) * gain)
    dk = norm_back(kraw_ref[...].astype(F32), dk_s[...])
    gp_s[:, 0:512] = dq.astype(BF16)
    gp_s[:, 512:1024] = dk.astype(BF16)
    gp_s[:, 1024:1536] = dv_s[...].astype(BF16)
    dnormed = mm_nt(gp_s[...], win_ref[...]) * scale
    r = lax.rsqrt(jnp.mean(x * x, axis=-1, keepdims=True) + 1e-06)
    along = jnp.mean(dnormed * x, axis=-1, keepdims=True)
    dx = r * dnormed - x * (r * r * r * along)
    dx_s[...] = (own_ref[128:256, :].astype(F32) + dx).astype(BF16)
    copies[1].start()

    for core in range(2):

        @pl.when(my_col % 2 == core)
        def _():
            keep_ref[:, 0:768] = gp_s[:, 768 * core : 768 * core + 768]
            keep_ref[:, 768:1024] = own_ref[128:256, 256 * core : 256 * core + 256]
            for j in range(8):
                at = slice(1024 + 128 * j, 1152 + 128 * j)
                if j < 6:
                    lane = 768 * (1 - core) + 128 * j
                    send_ref[at, :] = gp_s[:, lane : lane + 128]
                else:
                    lane = 256 * (1 - core) + 128 * (j - 6)
                    send_ref[at, :] = own_ref[128:256, lane : lane + 128]

    for copy in copies:
        copy.wait()


def grads_kernel(factor, sent_ref, keep_ref, got_ref, out_ref):
    features = jnp.concatenate([sent_ref[0:1024, :], got_ref[0:1024, :]], axis=1)
    got = jnp.concatenate([got_ref[1024 + 128 * j : 1152 + 128 * j, :] for j in range(8)], axis=1)
    grads = jnp.concatenate([keep_ref[...], got], axis=0)
    out_ref[:, 0:768] = (mm(features[:512], grads[:, :768]) * factor).astype(BF16)
    out_ref[:, 768:1024] = (mm(features[512:], grads[:, 768:]) * factor).astype(BF16)


def sum_kernel(rows, parts_ref, out_ref):
    count = parts_ref.shape[0] // rows
    step = max(rows, 16)
    total = parts_ref[0:step, :].astype(F32)
    for i in range(1, count * rows // step):
        total = total + parts_ref[step * i : step * (i + 1), :].astype(F32)
    while total.shape[0] > rows:
        half = total.shape[0] // 2
        total = total[:half] + total[half:]
    block = jnp.concatenate([total] * (step // rows), axis=0).astype(BF16)
    for i in range(count * rows // step):
        out_ref[step * i : step * (i + 1), :] = block


def final_kernel(mine, grads_ref, *refs):
    qkv_ref, out_ref, qkv_s, out_s, sems = refs[-5:]
    steps = sems.shape[1]
    rows = grads_ref.shape[0] // steps
    for core in range(2):

        @pl.when(lax.axis_index("cols") % 2 == core)
        def _():
            half = core if mine else 1 - core
            copies = []
            for i in range(steps):
                part = slice(rows * i, rows * (i + 1))
                qkv_s[part, :] = grads_ref[part, 0:768].astype(F32)
                out_s[part, :] = grads_ref[part, 768:1024].astype(F32)
                lanes = slice(768 * half, 768 * half + 768)
                copies.append(pltpu.make_async_copy(qkv_s.at[part], qkv_ref.at[part, lanes], sems.at[0, i]))
                lanes = slice(256 * half, 256 * half + 256)
                copies.append(pltpu.make_async_copy(out_s.at[part], out_ref.at[part, lanes], sems.at[1, i]))
                copies[-2].start()
                copies[-1].start()
            for copy in copies:
                copy.wait()


def write_half(mine, half_grads, *whole):
    unplaced = pl.BlockSpec(memory_space=pl.ANY)
    return pl.pallas_call(
        functools.partial(final_kernel, mine),
        in_specs=[pl.BlockSpec(memory_space=pltpu.VMEM)] + [unplaced] * len(whole),
        out_specs=[unplaced, unplaced],
        out_shape=[
            jax.ShapeDtypeStruct((512, 1536), F32),
            jax.ShapeDtypeStruct((512, 512), F32),
        ],
        scratch_shapes=[
            pltpu.VMEM((512, 768), F32), pltpu.VMEM((512, 256), F32), pltpu.SemaphoreType.DMA((2, 8)),
        ],
        input_output_aliases={1: 0, 2: 1} if whole else {},
        compiler_params=pltpu.CompilerParams(vmem_limit_bytes=SMALL_LIMIT),
        cost_estimate=pl.CostEstimate(flops=1 << 20, bytes_accessed=3 << 20, transcendentals=0),
    )(half_grads, *whole)


def call(kernel, outs, scratch=(), flops=0, scalars=0, inputs=0, unplaced_outs=0, limit=VMEM_LIMIT):
    whole = pl.BlockSpec(memory_space=pltpu.VMEM)
    return pl.pallas_call(
        kernel,
        out_shape=outs,
        in_specs=[pl.BlockSpec(memory_space=pltpu.SMEM)] * scalars
        + [whole] * inputs,
        out_specs=tuple(
            pl.BlockSpec(memory_space=pl.ANY) if i < unplaced_outs else whole for i in range(len(outs))
        )
        if isinstance(outs, tuple)
        else whole,
        scratch_shapes=list(scratch),
        compiler_params=pltpu.CompilerParams(vmem_limit_bytes=limit),
        cost_estimate=pl.CostEstimate(flops=flops, bytes_accessed=4 << 20, transcendentals=0),
    )


def condition(noise_level_step, label, category_gain_offset, noise_level_gain_matrix):
    half_freqs = noise_level_gain_matrix.shape[0] // 2
    steps_idx = jnp.arange(half_freqs, dtype=F32)
    freq_rates = 2.0 * math.pi * jnp.exp(steps_idx * (math.log(64.0) / half_freqs))
    angles = noise_level_step[0].astype(F32) * 0.001 * freq_rates
    features = jnp.concatenate([jnp.cos(angles), jnp.sin(angles)]).astype(BF16)
    shifted = jnp.dot(features[None, :], noise_level_gain_matrix, preferred_element_type=F32)
    class_row = lax.dynamic_slice_in_dim(category_gain_offset, label[0], 1, 0).astype(F32)
    return 1.0 + class_row + shifted


def swapped(value, row_to, col_to):
    n_rows, n_cols = lax.axis_size("rows"), lax.axis_size("cols")
    pairs = []
    for r in range(n_rows):
        for c in range(n_cols):
            to_row, to_col = row_to(r), col_to(c)
            if 0 <= to_row < n_rows and 0 <= to_col < n_cols:
                pairs.append((r * n_cols + c, to_row * n_cols + to_col))
    return lax.ppermute(value, AXES, pairs)


def same(i):
    return i


def paired(i):
    return i ^ 1


def across(i):
    return i - 1 if i % 2 == 0 else i + 1


def per_device(
    grid_token_states, upstream_gradient, noise_level_step, picture_category_label,
    category_gain_offset, noise_level_gain_matrix, attention_input_matrix,
    final_projection_matrix, cosine_logit_gain,
):
    x, du = grid_token_states, upstream_gradient
    height, columns, width = x.shape
    n_rows, n_cols = lax.axis_size("rows"), lax.axis_size("cols")
    tokens = height * columns
    bf = lambda *shape: jax.ShapeDtypeStruct(shape, BF16)
    vm = pltpu.VMEM
    own = jnp.concatenate([x, du], axis=0).reshape(2 * tokens, width)
    to_c, to_d, own = call(
        rows_kernel, (bf(144, width), bf(144, width), bf(256, width)), inputs=1, limit=SMALL_LIMIT
    )(own)
    from_c = swapped(to_c, paired, same)
    from_d = swapped(to_d, across, same)
    mate = swapped(own, same, paired)
    scale = condition(
        noise_level_step, picture_category_label, category_gain_offset, noise_level_gain_matrix
    )
    mask = call(
        mask_kernel,
        (jax.ShapeDtypeStruct((256, 128), jnp.int32), jax.ShapeDtypeStruct((256, 128), F32)),
        limit=SMALL_LIMIT,
    )()
    to_far, rows = call(
        columns_kernel, (bf(176, width), bf(288, width)), flops=16 << 30, inputs=7, limit=SMALL_LIMIT
    )(own, from_c, from_d, mate, scale, *mask)
    far = swapped(to_far, same, across)
    mate_rows = swapped(rows, same, paired)
    weights = (attention_input_matrix, final_projection_matrix, scale)
    k, v, q, do, kraw, qraw, normed = call(
        near_kernel,
        (bf(480, width), bf(480, width), bf(336, width), bf(336, width), bf(128, width), bf(128, width), bf(128, width)),
        scratch=[vm((320, 512), F32), vm((160, 512), F32), vm((336, 512), BF16)],
        flops=1 << 20, scalars=1, inputs=7,
    )(cosine_logit_gain, own, mate, rows, mate_rows, *weights)

    output, grad_latent, send, keep = call(
        main_kernel,
        (bf(tokens, width), bf(tokens, width), bf(2048, tokens), bf(tokens, 1024)),
        scratch=[
            vm((128, 512), BF16), vm((128, 512), BF16), pltpu.SemaphoreType.DMA((2,)),
            vm((160, 512), BF16), vm((160, 512), BF16), vm((112, 512), BF16), vm((112, 512), BF16),
            vm((128, 512), BF16), vm((128, 512), BF16), vm((128, 512), F32), vm((128, 512), F32),
            vm((128, 1536), BF16),
        ],
        flops=8 << 30, scalars=1, inputs=14, unplaced_outs=2,
    )(cosine_logit_gain, own, far, k, v, q, do, kraw, qraw, normed, *mask, *weights)

    got = swapped(send, same, paired)
    factor = 1.0 / math.sqrt(tokens * n_rows * n_cols)
    partial = call(
        functools.partial(grads_kernel, factor), bf(512, 1024), flops=1 << 29, inputs=3, limit=SMALL_LIMIT
    )(send, keep, got)

    groups = [
        [r * n_cols + 2 * c + core_ for r in range(n_rows) for c in range(n_cols // 2)]
        for core_ in range(2)
    ]
    members = n_rows * n_cols // 2
    each = 512 // members

    def exchange(value):
        return lax.all_to_all(
            value.reshape(members, each, 1024), AXES, 0, 0, axis_index_groups=groups, tiled=True
        ).reshape(512, 1024)

    summed = call(
        functools.partial(sum_kernel, each), bf(512, 1024), inputs=1, limit=SMALL_LIMIT
    )(exchange(partial))
    mine = exchange(summed)
    other = swapped(mine, same, paired)
    qkv_grad, out_grad = write_half(False, other, *write_half(True, mine))
    return output.reshape(x.shape), grad_latent.reshape(x.shape), qkv_grad, out_grad


def solution(mesh):
    placed = (P("rows", "cols", None), P("rows", "cols", None)) + (P(),) * 7
    return jax.shard_map(
        per_device,
        mesh=mesh,
        in_specs=placed,
        out_specs=(P("rows", "cols", None), P("rows", "cols", None), P(), P()),
        check_vma=False,
    )
```

```python
import functools
import math

import jax
import jax.numpy as jnp
from jax import lax
from jax.experimental import pallas as pl
from jax.experimental.pallas import tpu as pltpu
from jax.sharding import PartitionSpec as P

HEADS = 8
HEAD = 64
BF16 = jnp.bfloat16
F32 = jnp.float32
VMEM_LIMIT = 28 * 1024 * 1024
SMALL_LIMIT = 8 * 1024 * 1024
AXES = ("rows", "cols")
NEAR, FAR = 48, 16


def mm(a, b):
    return jnp.dot(a, b, preferred_element_type=F32)


def mm_nt(a, b):
    return lax.dot_general(a, b, (((1,), (1,)), ((), ())), preferred_element_type=F32)


def mm_tn(a, b):
    return lax.dot_general(a, b, (((0,), (0,)), ((), ())), preferred_element_type=F32)


def head_sums(product, ones):
    high = product.astype(BF16)
    low = (product - high.astype(F32)).astype(BF16)
    parts = []
    for g in range(2):
        lanes = slice(256 * g, 256 * g + 256)
        parts.append(mm(high[:, lanes], ones) + mm(low[:, lanes], ones))
    return jnp.concatenate(parts, axis=1)


def by_head(block):
    head_of = lax.broadcasted_iota(jnp.int32, block.shape, 1) // HEAD
    zero = jnp.zeros_like(block)
    return jnp.concatenate([jnp.where(head_of == h, block, zero) for h in range(4)], axis=0)


def own_heads(result):
    head_of = lax.broadcasted_iota(jnp.int32, (32, 256), 1) // HEAD
    total = result[:32]
    for h in range(1, 4):
        total = jnp.where(head_of == h, result[HEAD * h : HEAD * h + 32], total)
    return total


def head_ones():
    row_head = lax.broadcasted_iota(jnp.int32, (256, 256), 0) // HEAD
    lane_head = lax.broadcasted_iota(jnp.int32, (256, 256), 1) // HEAD
    return jnp.where(row_head == lane_head, 1.0, 0.0).astype(BF16)


def lane_gain(gain_ref):
    head_of = lax.broadcasted_iota(jnp.int32, (1, 512), 1) // HEAD
    gain = jnp.zeros((1, 512), F32)
    for h in range(HEADS):
        gain = jnp.where(head_of == h, gain_ref[h], gain)
    return gain


def block(ref, index):
    return ref[16 * index : 16 * index + 16, :].astype(F32)


def tile(ref, index):
    return block(ref, index // 2)[8 * (index % 2) : 8 * (index % 2) + 8]


def normalize(x, scale):
    return x * lax.rsqrt(jnp.mean(x * x, axis=-1, keepdims=True) + 1e-06) * scale


def unit(raw, ones):
    return raw * lax.rsqrt(head_sums(raw * raw, ones) + 1e-06)


def rows_kernel(own_ref, c_ref, d_ref, copy_ref):
    even = lax.axis_index("rows") % 2 == 0
    copy_ref[...] = own_ref[...]
    for ref, take_last in ((c_ref, even), (d_ref, jnp.logical_not(even))):

        @pl.when(take_last)
        def _():
            ref[0:96, :] = own_ref[32:128, :]
            ref[96:144, :] = own_ref[208:256, :]

        @pl.when(jnp.logical_not(take_last))
        def _():
            ref[0:96, :] = own_ref[0:96, :]
            ref[96:144, :] = own_ref[128:176, :]


def columns_kernel(own_ref, c_ref, d_ref, _mate, _scale, _row, _bias, far_ref, both_ref):
    even = lax.axis_index("rows") % 2 == 0
    first_core = lax.axis_index("cols") % 2 == 0
    sub = lax.broadcasted_iota(jnp.int32, (8, 512), 0)
    both_ref[0:144, :] = c_ref[...]
    both_ref[144:288, :] = d_ref[...]

    def x_edge(x):
        return jnp.where(first_core, x, pltpu.roll(x, 6, 0))[:8]

    def du_edge(du):
        third = jnp.where(first_core, du[2:3], du[15:16])
        return jnp.where(first_core, pltpu.roll(du, 6, 0), pltpu.roll(du, 9, 0))[:8], third

    tiles = []
    thirds = jnp.zeros((8, 512), F32)
    for row in range(8):
        two, third = du_edge(block(own_ref, 8 + row))
        tiles.append(jnp.where(sub < 6, x_edge(block(own_ref, row)), two))
        thirds = jnp.where(sub == row, third, thirds)
    tiles += [thirds, jnp.zeros((8, 512), F32)]
    for ref in (c_ref, d_ref):
        edges = [du_edge(block(ref, 6 + j)) for j in range(3)]
        for j in range(6):
            rest = edges[j][0] if j < 3 else edges[j - 3][1]
            tiles.append(jnp.where(sub < 6, x_edge(block(ref, j)), rest))
    for i in range(11):
        far_ref[16 * i : 16 * i + 16, :] = jnp.concatenate(tiles[2 * i : 2 * i + 2], 0).astype(BF16)


def near_kernel(
    gain_ref, own_ref, mate_ref, rows_ref, mate_rows_ref, win_ref, wo_ref, scale_ref,
    k_ref, v_ref, q_ref, do_ref, kraw_ref, qraw_ref, normed_ref,
    own_s, mate_s, du_s,
):
    even = lax.axis_index("rows") % 2 == 0
    first_core = lax.axis_index("cols") % 2 == 0
    scale = scale_ref[...]
    gain = lane_gain(gain_ref)
    ones = head_ones()

    def pick(low, high, above):
        return jnp.where(even, high, low) if above else jnp.where(even, low, high)

    def row_parts(row, first):
        if 0 <= row < 8:
            own, mate = block(own_ref, first + row), block(mate_ref, first + row)
        else:
            above = row < 0
            j = (row + (6 if above else -8)) if first == 0 else 6 + (row + (3 if above else -8))
            own = pick(block(rows_ref, j), block(rows_ref, 9 + j), above)
            mate = pick(block(mate_rows_ref, j), block(mate_rows_ref, 9 + j), above)
        return own, jnp.where(first_core, mate[:8], mate[8:])

    for e in range(20):
        own, mate = row_parts(e - 6, 0)
        own_s[16 * e : 16 * e + 16, :] = normalize(own, scale)
        mate_s[8 * e : 8 * e + 8, :] = normalize(mate, scale)
    normed_ref[...] = own_s[96:224, :].astype(BF16)
    for i in range(7):
        first, second = row_parts(2 * i - 3, 8), row_parts(2 * i - 2, 8)
        pair = jnp.concatenate([first[0], second[0], first[1], second[1]], axis=0)
        du_s[NEAR * i : NEAR * (i + 1), :] = pair.astype(BF16)

    def normed_pairs(first_row, count):
        parts = []
        for n in range(count):
            row = first_row + 2 * n
            parts += [own_s[16 * row : 16 * row + 32, :], mate_s[8 * row : 8 * row + 16, :]]
        return jnp.concatenate(parts, axis=0).astype(BF16)

    for t in range(5):
        rows = slice(96 * t, 96 * t + 96)
        normed = normed_pairs(4 * t, 2)
        raw = mm(normed, win_ref[:, 512:1024]).astype(BF16).astype(F32)
        k_ref[rows, :] = unit(raw, ones).astype(BF16)
        v_ref[rows, :] = mm(normed, win_ref[:, 1024:1536]).astype(BF16)
        for n in range(2):
            at = 2 * t + n - 3
            if 0 <= at < 4:
                kraw_ref[32 * at : 32 * at + 32, :] = raw[48 * n : 48 * n + 32].astype(BF16)
    for first, count in ((0, 2), (2, 2), (4, 2), (6, 1)):
        rows = slice(NEAR * first, NEAR * (first + count))
        normed = normed_pairs(3 + 2 * first, count)
        raw = mm(normed, win_ref[:, 0:512]).astype(BF16).astype(F32)
        q_ref[rows, :] = (unit(raw, ones) * gain).astype(BF16)
        do_ref[rows, :] = mm_nt(du_s[rows, :], wo_ref[...]).astype(BF16)
        for n in range(2 * count):
            at = 2 * first + n - 3
            if 0 <= at < 8:
                here = 48 * (n // 2) + 16 * (n % 2)
                qraw_ref[16 * at : 16 * at + 16, :] = raw[here : here + 16].astype(BF16)


def mask_kernel(row_ref, bias_ref):
    my_col = lax.axis_index("cols")
    first_core = my_col % 2 == 0
    mate_base = jnp.where(first_core, 16, -8)
    far_base = jnp.where(first_core, -6, 16)

    def places(index, near):
        in_near = index < near
        pair = jnp.where(in_near, index // NEAR, 0)
        j = jnp.where(in_near, index % NEAR, index - near)
        mine = in_near & (j < 32)
        eights = jnp.where(in_near, j - 32, j)
        row = jnp.where(mine, 2 * pair + j // 16, 2 * pair + eights // 8)
        slot = eights % 8
        far_col = jnp.where(slot < 6, far_base + slot, 1000)
        return row, jnp.where(mine, j % 16, jnp.where(in_near, mate_base + slot, far_col))

    key_row, key_col = places(lax.broadcasted_iota(jnp.int32, (256, 128), 0), 4 * NEAR)
    query_row, query_col = places(lax.broadcasted_iota(jnp.int32, (256, 128), 1) % 64, NEAR)
    row_gap, col_gap = key_row - query_row, key_col - query_col
    near = (row_gap >= 0) & (row_gap <= 6) & (col_gap >= -3) & (col_gap <= 3) & (key_col < 1000)
    image_col = key_col + 16 * my_col
    near = near & (image_col >= 0) & (image_col < 16 * lax.axis_size("cols"))
    row_ref[...] = key_row
    bias_ref[...] = jnp.where(near, 0.0, -1e30)


def main_kernel(
    gain_ref, own_ref, far_ref, kn_ref, vn_ref, qn_ref, don_ref, kraw_ref, qraw_ref, normed_ref,
    row_ref, bias_ref, win_ref, wo_ref, scale_ref,
    out_ref, dx_ref, send_ref, keep_ref,
    out_s, dx_s, sems, kf_s, vf_s, qf_s, dof_s, att_s, dq_s, dk_s, dv_s, gp_s,
):
    my_row, my_col = lax.axis_index("rows"), lax.axis_index("cols")
    even = my_row % 2 == 0
    first_core = my_col % 2 == 0
    scale = scale_ref[...]
    gain = lane_gain(gain_ref)
    ones = head_ones()
    sub = lax.broadcasted_iota(jnp.int32, (8, 512), 0)
    edge = jnp.where(first_core, 3, 0)

    def far_du(both, third):
        value = jnp.where(sub == edge, both[6:7], 0.0)
        value = jnp.where(sub == edge + 1, both[7:8], value)
        return jnp.where(sub == edge + 2, third, value)

    def rows_far(first_tile):
        return [tile(far_ref, first_tile + j) for j in range(6)]

    c_tiles, d_tiles = rows_far(10), rows_far(16)
    above = [jnp.where(even, d, c) for c, d in zip(c_tiles, d_tiles)]
    below = [jnp.where(even, c, d) for c, d in zip(c_tiles, d_tiles)]
    middle = [tile(far_ref, j) for j in range(8)]
    thirds = tile(far_ref, 8)
    x_far = jnp.concatenate(above + middle + below, axis=0)
    du_far = [far_du(above[j], above[j + 3][6:7]) for j in range(3)]
    du_far += [far_du(middle[j], thirds[j : j + 1]) for j in range(8)]
    du_far += [far_du(below[j], below[j + 3][6:7]) for j in range(3)]
    normed_far = normalize(x_far, scale)
    normed = normed_far.astype(BF16)
    raw = mm(normed, win_ref[:, 512:1024]).astype(BF16).astype(F32)
    kf_s[...] = unit(raw, ones).astype(BF16)
    vf_s[...] = mm(normed, win_ref[:, 1024:1536]).astype(BF16)
    raw = mm(normed_far[24:136].astype(BF16), win_ref[:, 0:512]).astype(BF16).astype(F32)
    qf_s[...] = (unit(raw, ones) * gain).astype(BF16)
    dof_s[...] = mm_nt(jnp.concatenate(du_far, axis=0).astype(BF16), wo_ref[...]).astype(BF16)

    dk_s[...] = jnp.zeros_like(dk_s)
    dv_s[...] = jnp.zeros_like(dv_s)
    for i in range(7):
        image_row = row_ref[...] + (8 * my_row - 6 + 2 * i)
        inside = (image_row >= 0) & (image_row < 8 * lax.axis_size("rows"))
        bias = jnp.where(inside, bias_ref[...], -1e30)
        bias = jnp.concatenate([bias, bias], axis=1)
        blocks = range(max(i, 3), min(i + 4, 7))
        there = slice(32 * (blocks[0] - 3), 32 * (blocks[-1] - 2))

        def own_keys(value):
            parts = [value[NEAR * (b - i) : NEAR * (b - i) + 32] for b in blocks]
            return jnp.concatenate(parts, axis=0)

        for g in range(2):
            lanes = slice(256 * g, 256 * g + 256)

            def keys(near_ref, far_ref):
                parts = [near_ref[NEAR * i : NEAR * (i + 4), lanes], far_ref[FAR * i : FAR * (i + 4), lanes]]
                return jnp.concatenate(parts, axis=0)

            def queries(near_ref, far_ref):
                parts = [near_ref[NEAR * i : NEAR * (i + 1), lanes], far_ref[FAR * i : FAR * (i + 1), lanes]]
                return by_head(jnp.concatenate(parts, axis=0))

            k_t, v_t = keys(kn_ref, kf_s), keys(vn_ref, vf_s)
            q_h, do_h = queries(qn_ref, qf_s), queries(don_ref, dof_s)
            scores = mm_nt(k_t, q_h) + bias
            weight = jnp.exp(scores - jnp.max(scores, axis=0, keepdims=True))
            weight = weight * (1.0 / jnp.sum(weight, axis=0, keepdims=True))
            prob = weight.astype(BF16)
            dprob = mm_nt(v_t, do_h)
            mean = jnp.sum(weight * dprob, axis=0, keepdims=True)
            dscore = (weight * (dprob - mean)).astype(BF16)
            dv_s[there, lanes] += mm(own_keys(prob), do_h)
            dk_s[there, lanes] += mm(own_keys(dscore), q_h)
            if 1 <= i <= 5:
                att = own_heads(mm_tn(prob, v_t)).astype(BF16)
                dq = own_heads(mm_tn(dscore, k_t)).astype(BF16)
                for n in range(2):
                    at = 2 * i + n - 3
                    if 0 <= at < 8:
                        att_s[16 * at : 16 * at + 16, lanes] = att[16 * n : 16 * n + 16]
                        dq_s[16 * at : 16 * at + 16, lanes] = dq[16 * n : 16 * n + 16]

    att = att_s[...]
    normed = normed_ref[...]
    x = own_ref[0:128, :].astype(F32)
    out_s[...] = (x + mm(att, wo_ref[...])).astype(BF16)
    copies = [pltpu.make_async_copy(out_s, out_ref, sems.at[0]), pltpu.make_async_copy(dx_s, dx_ref, sems.at[1])]
    copies[0].start()
    send_ref[0:512, :] = jnp.transpose(normed)
    send_ref[512:1024, :] = jnp.transpose(att)

    def norm_back(raw, grad):
        inv = lax.rsqrt(head_sums(raw * raw, ones) + 1e-06)
        return inv * (grad - raw * (inv * inv) * head_sums(raw * grad, ones))

    dq = norm_back(qraw_ref[...].astype(F32), dq_s[...].astype(F32) * gain)
    dk = norm_back(kraw_ref[...].astype(F32), dk_s[...])
    gp_s[:, 0:512] = dq.astype(BF16)
    gp_s[:, 512:1024] = dk.astype(BF16)
    gp_s[:, 1024:1536] = dv_s[...].astype(BF16)
    dnormed = mm_nt(gp_s[...], win_ref[...]) * scale
    r = lax.rsqrt(jnp.mean(x * x, axis=-1, keepdims=True) + 1e-06)
    along = jnp.mean(dnormed * x, axis=-1, keepdims=True)
    dx = r * dnormed - x * (r * r * r * along)
    dx_s[...] = (own_ref[128:256, :].astype(F32) + dx).astype(BF16)
    copies[1].start()

    for core in range(2):

        @pl.when(my_col % 2 == core)
        def _():
            keep_ref[:, 0:768] = gp_s[:, 768 * core : 768 * core + 768]
            keep_ref[:, 768:1024] = own_ref[128:256, 256 * core : 256 * core + 256]
            for j in range(8):
                at = slice(1024 + 128 * j, 1152 + 128 * j)
                if j < 6:
                    lane = 768 * (1 - core) + 128 * j
                    send_ref[at, :] = gp_s[:, lane : lane + 128]
                else:
                    lane = 256 * (1 - core) + 128 * (j - 6)
                    send_ref[at, :] = own_ref[128:256, lane : lane + 128]

    for copy in copies:
        copy.wait()


def grads_kernel(factor, sent_ref, keep_ref, got_ref, out_ref):
    features = jnp.concatenate([sent_ref[0:1024, :], got_ref[0:1024, :]], axis=1)
    got = jnp.concatenate([got_ref[1024 + 128 * j : 1152 + 128 * j, :] for j in range(8)], axis=1)
    grads = jnp.concatenate([keep_ref[...], got], axis=0)
    out_ref[:, 0:768] = (mm(features[:512], grads[:, :768]) * factor).astype(BF16)
    out_ref[:, 768:1024] = (mm(features[512:], grads[:, 768:]) * factor).astype(BF16)


def sum_kernel(rows, parts_ref, out_ref):
    count = parts_ref.shape[0] // rows
    step = max(rows, 16)
    total = parts_ref[0:step, :].astype(F32)
    for i in range(1, count * rows // step):
        total = total + parts_ref[step * i : step * (i + 1), :].astype(F32)
    while total.shape[0] > rows:
        half = total.shape[0] // 2
        total = total[:half] + total[half:]
    block = jnp.concatenate([total] * (step // rows), axis=0).astype(BF16)
    for i in range(count * rows // step):
        out_ref[step * i : step * (i + 1), :] = block


def final_kernel(mine, first, grads_ref, *refs):
    qkv_ref, out_ref, qkv_s, out_s, sems = refs[-5:]
    steps = sems.shape[1]
    rows = grads_ref.shape[0] // steps
    for core in range(2):

        @pl.when(lax.axis_index("cols") % 2 == core)
        def _():
            half = core if mine else 1 - core
            copies = []
            for i in range(steps):
                part = slice(rows * i, rows * (i + 1))
                qkv_s[part, :] = grads_ref[part, 0:768].astype(F32)
                out_s[part, :] = grads_ref[part, 768:1024].astype(F32)
                there = slice(first + rows * i, first + rows * (i + 1))
                lanes = slice(768 * half, 768 * half + 768)
                copies.append(pltpu.make_async_copy(qkv_s.at[part], qkv_ref.at[there, lanes], sems.at[0, i]))
                lanes = slice(256 * half, 256 * half + 256)
                copies.append(pltpu.make_async_copy(out_s.at[part], out_ref.at[there, lanes], sems.at[1, i]))
                copies[-2].start()
                copies[-1].start()
            for copy in copies:
                copy.wait()


def write_half(mine, first, half_grads, *whole):
    unplaced = pl.BlockSpec(memory_space=pl.ANY)
    return pl.pallas_call(
        functools.partial(final_kernel, mine, first),
        in_specs=[pl.BlockSpec(memory_space=pltpu.VMEM)] + [unplaced] * len(whole),
        out_specs=[unplaced, unplaced],
        out_shape=[
            jax.ShapeDtypeStruct((512, 1536), F32),
            jax.ShapeDtypeStruct((512, 512), F32),
        ],
        scratch_shapes=[
            pltpu.VMEM((512, 768), F32), pltpu.VMEM((512, 256), F32), pltpu.SemaphoreType.DMA((2, 8)),
        ],
        input_output_aliases={1: 0, 2: 1} if whole else {},
        compiler_params=pltpu.CompilerParams(vmem_limit_bytes=SMALL_LIMIT),
        cost_estimate=pl.CostEstimate(flops=1 << 20, bytes_accessed=3 << 20, transcendentals=0),
    )(half_grads, *whole)


def call(kernel, outs, scratch=(), flops=0, scalars=0, inputs=0, unplaced_outs=0, limit=VMEM_LIMIT):
    whole = pl.BlockSpec(memory_space=pltpu.VMEM)
    return pl.pallas_call(
        kernel,
        out_shape=outs,
        in_specs=[pl.BlockSpec(memory_space=pltpu.SMEM)] * scalars
        + [whole] * inputs,
        out_specs=tuple(
            pl.BlockSpec(memory_space=pl.ANY) if i < unplaced_outs else whole for i in range(len(outs))
        )
        if isinstance(outs, tuple)
        else whole,
        scratch_shapes=list(scratch),
        compiler_params=pltpu.CompilerParams(vmem_limit_bytes=limit),
        cost_estimate=pl.CostEstimate(flops=flops, bytes_accessed=4 << 20, transcendentals=0),
    )


def condition(noise_level_step, label, category_gain_offset, noise_level_gain_matrix):
    half_freqs = noise_level_gain_matrix.shape[0] // 2
    steps_idx = jnp.arange(half_freqs, dtype=F32)
    freq_rates = 2.0 * math.pi * jnp.exp(steps_idx * (math.log(64.0) / half_freqs))
    angles = noise_level_step[0].astype(F32) * 0.001 * freq_rates
    features = jnp.concatenate([jnp.cos(angles), jnp.sin(angles)]).astype(BF16)
    shifted = jnp.dot(features[None, :], noise_level_gain_matrix, preferred_element_type=F32)
    class_row = lax.dynamic_slice_in_dim(category_gain_offset, label[0], 1, 0).astype(F32)
    return 1.0 + class_row + shifted


def swapped(value, row_to, col_to):
    n_rows, n_cols = lax.axis_size("rows"), lax.axis_size("cols")
    pairs = []
    for r in range(n_rows):
        for c in range(n_cols):
            to_row, to_col = row_to(r), col_to(c)
            if 0 <= to_row < n_rows and 0 <= to_col < n_cols:
                pairs.append((r * n_cols + c, to_row * n_cols + to_col))
    return lax.ppermute(value, AXES, pairs)


def same(i):
    return i


def paired(i):
    return i ^ 1


def across(i):
    return i - 1 if i % 2 == 0 else i + 1


def per_device(
    grid_token_states, upstream_gradient, noise_level_step, picture_category_label,
    category_gain_offset, noise_level_gain_matrix, attention_input_matrix,
    final_projection_matrix, cosine_logit_gain,
):
    x, du = grid_token_states, upstream_gradient
    height, columns, width = x.shape
    n_rows, n_cols = lax.axis_size("rows"), lax.axis_size("cols")
    tokens = height * columns
    bf = lambda *shape: jax.ShapeDtypeStruct(shape, BF16)
    vm = pltpu.VMEM
    own = jnp.concatenate([x, du], axis=0).reshape(2 * tokens, width)
    to_c, to_d, own = call(
        rows_kernel, (bf(144, width), bf(144, width), bf(256, width)), inputs=1, limit=SMALL_LIMIT
    )(own)
    from_c = swapped(to_c, paired, same)
    from_d = swapped(to_d, across, same)
    mate = swapped(own, same, paired)
    scale = condition(
        noise_level_step, picture_category_label, category_gain_offset, noise_level_gain_matrix
    )
    mask = call(
        mask_kernel,
        (jax.ShapeDtypeStruct((256, 128), jnp.int32), jax.ShapeDtypeStruct((256, 128), F32)),
        limit=SMALL_LIMIT,
    )()
    to_far, rows = call(
        columns_kernel, (bf(176, width), bf(288, width)), flops=16 << 30, inputs=7, limit=SMALL_LIMIT
    )(own, from_c, from_d, mate, scale, *mask)
    far = swapped(to_far, same, across)
    mate_rows = swapped(rows, same, paired)
    weights = (attention_input_matrix, final_projection_matrix, scale)
    k, v, q, do, kraw, qraw, normed = call(
        near_kernel,
        (bf(480, width), bf(480, width), bf(336, width), bf(336, width), bf(128, width), bf(128, width), bf(128, width)),
        scratch=[vm((320, 512), F32), vm((160, 512), F32), vm((336, 512), BF16)],
        flops=1 << 20, scalars=1, inputs=7,
    )(cosine_logit_gain, own, mate, rows, mate_rows, *weights)

    output, grad_latent, send, keep = call(
        main_kernel,
        (bf(tokens, width), bf(tokens, width), bf(2048, tokens), bf(tokens, 1024)),
        scratch=[
            vm((128, 512), BF16), vm((128, 512), BF16), pltpu.SemaphoreType.DMA((2,)),
            vm((160, 512), BF16), vm((160, 512), BF16), vm((112, 512), BF16), vm((112, 512), BF16),
            vm((128, 512), BF16), vm((128, 512), BF16), vm((128, 512), F32), vm((128, 512), F32),
            vm((128, 1536), BF16),
        ],
        flops=8 << 30, scalars=1, inputs=14, unplaced_outs=2,
    )(cosine_logit_gain, own, far, k, v, q, do, kraw, qraw, normed, *mask, *weights)

    got = swapped(send, same, paired)
    factor = 1.0 / math.sqrt(tokens * n_rows * n_cols)
    partial = call(
        functools.partial(grads_kernel, factor), bf(512, 1024), flops=1 << 29, inputs=3, limit=SMALL_LIMIT
    )(send, keep, got)

    groups = [
        [r * n_cols + 2 * c + core_ for r in range(n_rows) for c in range(n_cols // 2)]
        for core_ in range(2)
    ]
    members = n_rows * n_cols // 2
    each = 512 // members

    def exchange(value):
        return lax.all_to_all(
            value.reshape(members, each, 1024), AXES, 0, 0, axis_index_groups=groups, tiled=True
        ).reshape(512, 1024)

    summed = call(
        functools.partial(sum_kernel, each), bf(512, 1024), inputs=1, limit=SMALL_LIMIT
    )(exchange(partial))
    mine = exchange(summed)
    upper, lower = swapped(mine[:256], same, paired), swapped(mine[256:], same, paired)
    grads = write_half(True, 0, mine)
    grads = write_half(False, 0, upper, *grads)
    qkv_grad, out_grad = write_half(False, 256, lower, *grads)
    return output.reshape(x.shape), grad_latent.reshape(x.shape), qkv_grad, out_grad


def solution(mesh):
    placed = (P("rows", "cols", None), P("rows", "cols", None)) + (P(),) * 7
    return jax.shard_map(
        per_device,
        mesh=mesh,
        in_specs=placed,
        out_specs=(P("rows", "cols", None), P("rows", "cols", None), P(), P()),
        check_vma=False,
    )
```
